32 devices in a mesh: dom: 4 (over x, core), blk: 8 (over z, y).
Axes of the slice: x: 2, y: 2, z: 4, core: 2. Of those that a mesh axis runs over, the one named last changes fastest.
Arguments:
- incident: bfloat16 [256, 512, 192], P(('dom', 'blk')), may hold values from -6 to 6
- t_matrices: bfloat16 [256, 512, 512], P(('dom', 'blk')), may hold values from -0.25 to 0.25
- translations: bfloat16 [4, 512, 512], replicated, may hold values from -0.125 to 0.125
- near_index: int32 [256, 6], P(('dom', 'blk')), may hold values from 0 to 255, as said below
- near_count: int32 [256], P(('dom', 'blk')), may hold values from 1 to 6, as said below
- near_type: int32 [256, 6], P(('dom', 'blk')), may hold values from 0 to 3
- phases: bfloat16 [256, 2048], P(('dom', 'blk')), may hold values from -1 to 1
- wave_basis: bfloat16 [2048, 512], replicated, may hold values from -0.25 to 0.25
- grating_blocks: float32 [16, 128, 128], P('blk'), may hold values from -0.0234375 to 0.0234375
Outputs:
- coeffs: bfloat16 [256, 512, 192], P(('dom', 'blk'))
The draws below stay inside these ranges and needn't reach their ends.
Inputs may be any that keep to these rules, and one draw needn't show every extreme that they name: `near_index`: the first near_count[p] entries of row p are distinct particles other than p, each within 4 of p, ascending; the remaining entries equal p and carry no weight. `near_count`: some particle has exactly 6 live neighbours.
All inputs are finite; a program needn't handle non-finite values.
Results may differ from the reference program's by a relative error of at most 0.015.
Values may be sent and summed in bfloat16 or wider, within the bound.
No kernel may reach another device: no remote copies, remote signals or barrier semaphores. Data moves between devices by JAX's collectives and lax.ppermute only.
A program may use at most 64 MiB of HBM per device.

```python
import math
import jax
import jax.numpy as jnp
from jax import lax

L = 512
M = 192
G = 2048
BLOCK = 128
NT = 4
K = 6
ITERS = 2
REACH = 4
P_SIZE = 256
NB = 16


def near_lists(key):
    first_key, second_key, third_key = jax.random.split(jax.random.fold_in(key, 7), 3)
    offsets = jnp.concatenate([jnp.arange(-REACH, 0), jnp.arange(1, REACH + 1)]).astype(jnp.int32)
    particle = jnp.arange(P_SIZE, dtype=jnp.int32)[:, None]
    candidate = particle + offsets[None, :]
    valid = (candidate >= 0) & (candidate < P_SIZE)
    valid_count = jnp.sum(valid.astype(jnp.int32), axis=1)
    raw_score = jax.random.randint(first_key, (P_SIZE, 2 * REACH), 0, 1 << 20)
    positions = jnp.arange(2 * REACH, dtype=jnp.int32)[None, :]
    score = jnp.where(valid, raw_score * (2 * REACH) + positions, -1 - positions)
    ranking = jnp.argsort(-score, axis=1, stable=True)
    counts = jax.random.randint(second_key, (P_SIZE,), 1, K + 1)
    forced = jax.random.randint(third_key, (), REACH, P_SIZE - REACH)
    counts = jnp.where(particle[:, 0] == forced, K, counts)
    counts = jnp.minimum(counts, valid_count)
    chosen = jnp.take_along_axis(candidate, ranking[:, :K], axis=1)
    live = jnp.arange(K, dtype=jnp.int32)[None, :] < counts[:, None]
    keyed = jnp.where(live, chosen, 2 * P_SIZE + jnp.arange(K, dtype=jnp.int32)[None, :])
    keyed = jnp.sort(keyed, axis=1)
    index = jnp.where(keyed < P_SIZE, keyed, particle)
    return (index.astype(jnp.int32), counts.astype(jnp.int32))


def draw_near_index(key, part):
    return near_lists(key)[0]


def draw_near_count(key, part):
    return near_lists(key)[1]


def set_ends(result, rng, low, top_value):
    longest = result.shape.index(max(result.shape))
    spots = []
    for shift in (0, 1):
        where = [jax.random.randint(jax.random.fold_in(rng, axis), (), 0, length) for axis, length in enumerate(result.shape)]
        where[longest] = (where[longest] + shift) % result.shape[longest]
        spots.append(tuple(where))
    return result.at[spots[0]].set(low).at[spots[1]].set(top_value)


def level_of(own_key, dims, cuts, least, high):
    loudness, own = 1.0, jax.random.fold_in(own_key, 6)
    for dim, blocks in cuts:
        steps = jnp.exp(jax.random.uniform(jax.random.fold_in(own, dim), (blocks,), jnp.float32, least / len(cuts), high / len(cuts)))
        loudness = loudness * jnp.repeat(steps, dims[dim] // blocks).reshape([-1 if axis == dim else 1 for axis in range(len(dims))])
    return loudness


def gaussian(own_key, extent, width, reach, cuts=(), kind=jnp.bfloat16):
    entries = jax.random.normal(own_key, extent, jnp.float32) * width
    if len(cuts) > 0:
        entries = level_of(own_key, extent, cuts, -0.22, 0.18) * entries
    return jnp.clip(entries, min=-reach, max=reach).astype(kind)


def setup_inputs(seed: int = 0) -> dict:
    key_list = jax.random.split(jax.random.key(seed), 10)
    return {
        "incident": gaussian(key_list[0], (P_SIZE, L, M), 1.0, 6.0, ((0, 32),)),
        "t_matrices": gaussian(key_list[1], (P_SIZE, L, L), L ** -0.5, 0.25, ((0, 32),)),
        "translations": gaussian(key_list[2], (NT, L, L), (4 * L) ** -0.5, 0.125),
        "near_index": draw_near_index(jax.random.fold_in(key_list[9], 71), 0),
        "near_count": draw_near_count(jax.random.fold_in(key_list[9], 71), 0),
        "near_type": set_ends(jax.random.randint(key_list[5], (P_SIZE, K), 0, NT), jax.random.fold_in(key_list[5], 1), 0, NT - 1).astype(jnp.int32),
        "phases": jnp.clip(jax.random.uniform(key_list[6], (P_SIZE, G), jnp.float32, -1.0, 1.0) * level_of(key_list[6], (P_SIZE, G), ((0, 32),), -0.4, 0.0), -1.0, 1.0).astype(jnp.bfloat16),
        "wave_basis": gaussian(key_list[7], (G, L), L ** -0.5, 0.25),
        "grating_blocks": gaussian(key_list[8], (NB, BLOCK, BLOCK), (2 * BLOCK * P_SIZE) ** -0.5, 0.0234375, ((0, 8),), jnp.float32),
    }


def rounded(values):
    return lax.optimization_barrier(values.astype(jnp.bfloat16)).astype(jnp.float32)


def solve_block(t_block, source):
    return jnp.einsum('pab,pbm->pam', t_block.astype(jnp.float32), source.astype(jnp.float32)).astype(jnp.bfloat16)


def reference(incident, t_matrices, translations, near_index, near_count, near_type, phases, wave_basis, grating_blocks):
    blocks = math.gcd(P_SIZE, 64)
    groups = P_SIZE // blocks

    def shaped(values):
        return values.reshape((groups, blocks) + values.shape[1:])

    basis = wave_basis.astype(jnp.float32)
    moves = translations.astype(jnp.float32)
    coeffs = lax.map(lambda pair: solve_block(pair[0], pair[1]), (shaped(t_matrices), shaped(incident))).reshape(P_SIZE, L, M)
    live = jnp.arange(K)[None, :] < near_count[:, None]
    for sweep in range(ITERS):
        def outward(total, pair):
            phase_block, coeff_block = pair
            spread = jnp.einsum('gl,plm->pgm', basis, coeff_block.astype(jnp.float32))
            return total + jnp.einsum('pg,pgm->gm', phase_block.astype(jnp.float32), spread), None

        sums, _ = lax.scan(outward, jnp.zeros((G, M), jnp.float32), (shaped(phases), shaped(coeffs)))
        reflected = jnp.einsum('bij,bjm->bim', grating_blocks.astype(jnp.float32), sums.reshape(NB, BLOCK, M), precision=lax.Precision.HIGHEST).reshape(G, M)
        reflected_wide = rounded(reflected)
        current = coeffs

        def update(items):
            t_block, inc_block, index_block, live_block, type_block, phase_block = items
            gathered = jnp.take(current, index_block, axis=0).astype(jnp.float32)
            weights = ((type_block[None] == jnp.arange(NT)[:, None, None]) & live_block[None]).astype(jnp.float32)
            grouped = rounded(jnp.einsum('tpk,pklm->tplm', weights, gathered))
            near_field = jnp.einsum('tab,tpbm->pam', moves, grouped)
            weighted = rounded(phase_block.astype(jnp.float32)[:, :, None] * reflected_wide[None])
            returned = jnp.einsum('gl,pgm->plm', basis, weighted)
            source = rounded(inc_block.astype(jnp.float32) + near_field + returned)
            return solve_block(t_block, source)

        coeffs = lax.map(update, (shaped(t_matrices), shaped(incident), shaped(near_index), shaped(live), shaped(near_type), shaped(phases))).reshape(P_SIZE, L, M)
    return coeffs
```

```python
import jax
import jax.numpy as jnp
from jax import lax
from jax.experimental import pallas as pl
from jax.experimental.pallas import tpu as pltpu
from jax.sharding import PartitionSpec as P

ITERS = 2
AXES = ("dom", "blk")
F32 = jnp.float32
BF16 = jnp.bfloat16
LAST = (((1,), (1,)), ((), ()))
MIB = 1 << 20


def params(mib):
    return pltpu.CompilerParams(vmem_limit_bytes=mib * MIB)


def cost(macs, moved):
    return pl.CostEstimate(flops=2 * macs, bytes_accessed=moved, transcendentals=0)


def solve_kernel(source_ref, t_ref, out_ref):
    out_ref[0] = lax.dot_general(
        source_ref[0], t_ref[0], LAST, preferred_element_type=F32
    ).astype(BF16)


def solve(source, t_matrices, start, count):
    m, size = source.shape[1:]
    return pl.pallas_call(
        solve_kernel,
        grid=(count,),
        in_specs=[
            pl.BlockSpec((1, m, size), lambda p: (start + p, 0, 0)),
            pl.BlockSpec((1, size, size), lambda p: (start + p, 0, 0)),
        ],
        out_specs=pl.BlockSpec((1, m, size), lambda p: (p, 0, 0)),
        out_shape=jax.ShapeDtypeStruct((count, m, size), BF16),
        compiler_params=params(16),
        cost_estimate=cost(count * m * size * size, 2 * count * size * (2 * m + size)),
        name="solve",
    )(source, t_matrices)


def outward_kernel(part_ref, low_ref, high_ref, basis_ref, phase_ref, out_ref):
    half, rows, size = low_ref.shape
    width = basis_ref.shape[0]
    total = jnp.zeros((rows, width), F32)
    for index, ref in ((0, low_ref), (half, high_ref)):
        spread = lax.dot_general(
            ref[...].reshape(half * rows, size),
            basis_ref[...],
            LAST,
            preferred_element_type=F32,
        )
        for p in range(half):
            phase = phase_ref[index + p, :].astype(F32)[None, :]
            total = total + phase * spread[p * rows : (p + 1) * rows]
    out_ref[0] = total.astype(BF16)


def outward(part, low, high, basis, phases, parts, chunks):
    half, m, size = low.shape
    total_rows = basis.shape[0]
    width = total_rows // chunks
    rows = m // parts
    return pl.pallas_call(
        outward_kernel,
        grid_spec=pltpu.PrefetchScalarGridSpec(
            num_scalar_prefetch=1,
            grid=(chunks,),
            in_specs=[
                pl.BlockSpec((half, rows, size), lambda g, part: (0, part[0], 0)),
                pl.BlockSpec((half, rows, size), lambda g, part: (0, part[0], 0)),
                pl.BlockSpec((width, size), lambda g, part: (g, 0)),
                pl.BlockSpec((2 * half, width), lambda g, part: (0, g)),
            ],
            out_specs=pl.BlockSpec((1, rows, width), lambda g, part: (g, 0, 0)),
        ),
        out_shape=jax.ShapeDtypeStruct((chunks, rows, width), BF16),
        compiler_params=params(24),
        cost_estimate=cost(
            2 * half * rows * size * total_rows, 2 * size * (total_rows + 2 * half * rows)
        ),
        name="outward",
    )(part, low, high, basis, phases)


def near_kernel(
    slot_ref,
    count_ref,
    type_ref,
    before_ref,
    low_ref,
    high_ref,
    after_ref,
    incident_ref,
    translations_ref,
    out_ref,
    extended,
    sums,
):
    group, m, size = incident_ref.shape
    reach = low_ref.shape[0]
    kinds = translations_ref.shape[0]
    most = slot_ref.shape[1]
    step = pl.program_id(0)

    @pl.when(step == 0)
    def _():
        for index, ref in enumerate((before_ref, low_ref, high_ref, after_ref)):
            extended[pl.ds(index * reach, reach)] = ref[...]

    sums[...] = jnp.zeros(sums.shape, F32)
    for i in range(group):
        p = step * group + i
        for k in range(most):

            @pl.when(k < count_ref[p])
            def _():
                place = type_ref[p, k]
                sums[place, i] += extended[slot_ref[p, k]].astype(F32)

    total = incident_ref[...].astype(F32).reshape(group * m, size)
    for t in range(kinds):
        total = total + lax.dot_general(
            sums[t].astype(BF16).reshape(group * m, size),
            translations_ref[t],
            LAST,
            preferred_element_type=F32,
        )
    out_ref[...] = total.reshape(group, m, size)


def near(slots, counts, types, before, low, high, after, incident, translations):
    count, m, size = incident.shape
    reach = low.shape[0]
    kinds = translations.shape[0]
    group = 4
    whole = pl.BlockSpec((reach, m, size), lambda p, *_: (0, 0, 0))
    return pl.pallas_call(
        near_kernel,
        grid_spec=pltpu.PrefetchScalarGridSpec(
            num_scalar_prefetch=3,
            grid=(count // group,),
            in_specs=[
                whole,
                whole,
                whole,
                whole,
                pl.BlockSpec((group, m, size), lambda p, *_: (p, 0, 0)),
                pl.BlockSpec((kinds, size, size), lambda p, *_: (0, 0, 0)),
            ],
            out_specs=pl.BlockSpec((group, m, size), lambda p, *_: (p, 0, 0)),
            scratch_shapes=[
                pltpu.VMEM((4 * reach, m, size), BF16),
                pltpu.VMEM((kinds, group, m, size), F32),
            ],
        ),
        out_shape=jax.ShapeDtypeStruct((count, m, size), F32),
        compiler_params=params(40),
        cost_estimate=cost(kinds * count * m * size * size, 2 * size * size * kinds),
        name="near",
    )(slots, counts, types, before, low, high, after, incident, translations)


def back_kernel(phase_ref, waves_ref, basis_ref, partial_ref, t_ref, out_ref):
    group, m, size = partial_ref.shape
    chunks, _, width = waves_ref.shape
    total = partial_ref[...].reshape(group * m, size)
    for c in range(chunks):
        weighted = []
        for i in range(group):
            weighted.append(phase_ref[i, :, pl.ds(c * width, width)] * waves_ref[c])
        total = total + jnp.dot(
            jnp.concatenate(weighted, axis=0),
            basis_ref[pl.ds(c * width, width), :],
            preferred_element_type=F32,
        )
    source = total.astype(BF16)
    for i in range(group):
        out_ref[i] = lax.dot_general(
            source[i * m : (i + 1) * m], t_ref[i], LAST, preferred_element_type=F32
        ).astype(BF16)


def back(phases, waves, basis, partial, t_matrices, start, count):
    chunks, m, width = waves.shape
    size = basis.shape[1]
    total_rows = basis.shape[0]
    group = 2
    first = start // group
    return pl.pallas_call(
        back_kernel,
        grid=(count // group,),
        in_specs=[
            pl.BlockSpec((group, 1, total_rows), lambda p: (first + p, 0, 0)),
            pl.BlockSpec((chunks, m, width), lambda p: (0, 0, 0)),
            pl.BlockSpec((total_rows, size), lambda p: (0, 0)),
            pl.BlockSpec((group, m, size), lambda p: (first + p, 0, 0)),
            pl.BlockSpec((group, size, size), lambda p: (first + p, 0, 0)),
        ],
        out_specs=pl.BlockSpec((group, m, size), lambda p: (p, 0, 0)),
        out_shape=jax.ShapeDtypeStruct((count, m, size), BF16),
        compiler_params=params(32),
        cost_estimate=cost(
            count * m * size * (total_rows + size), 2 * size * (total_rows + count * size)
        ),
        name="back",
    )(phases[:, None, :], waves, basis, partial, t_matrices)


def add(*terms):
    total = terms[0].astype(F32)
    for term in terms[1:]:
        total = total + term.astype(F32)
    return total.astype(BF16)


def local(
    incident,
    t_matrices,
    translations,
    near_index,
    near_count,
    near_type,
    phases,
    wave_basis,
    grating_blocks,
):
    doms, blks = lax.axis_size("dom"), lax.axis_size("blk")
    devices = doms * blks
    x_count, z_count = doms // 2, min(4, blks)
    y_count = blks // z_count
    count, size, m = incident.shape
    reach = count // 2
    me = lax.axis_index(AXES)
    core = lax.axis_index("dom") % 2
    x = lax.axis_index("dom") // 2
    z = lax.axis_index("blk") // y_count
    y = lax.axis_index("blk") % y_count

    def flip(array, mask):
        return lax.ppermute(array, AXES, [(i, i ^ mask) for i in range(devices)])

    def mask_of(dx, dy):
        return dx * 2 * blks + dy

    core_mask = blks
    plane = [
        (dx, dy) for dx in range(x_count) for dy in range(y_count) if (dx, dy) != (0, 0)
    ]
    plane.sort(key=lambda pair: -(pair[0] > 0) - (pair[1] > 0))
    column = [d for d in (2, 3, 1) if d < z_count]

    def reduce_reflect_gather(send, keep):
        width = keep.shape[2]
        rows = m // 2 // x_count
        got = flip(send, core_mask)
        split = (z_count, y_count, x_count, rows, width)

        def shaped(array):
            return array.reshape(blks, x_count, rows, width).reshape(split)

        def part(array, at_x, at_y):
            return lax.dynamic_slice(
                array, (0, at_y, at_x, 0, 0), (z_count, 1, 1, rows, width)
            )[:, 0, 0]

        keep, got = shaped(keep), shaped(got)

        def summed(at_x, at_y):
            return add(part(keep, at_x, at_y), part(got, at_x, at_y))

        arrived = [flip(summed(x ^ dx, y ^ dy), mask_of(dx, dy)) for dx, dy in plane]
        plane_sum = add(part(keep, x, y), part(got, x, y), *arrived)

        def row(at_z):
            return lax.dynamic_slice_in_dim(plane_sum, at_z, 1, axis=0)[0]

        arrived = [flip(row(z ^ dz), dz * y_count) for dz in column]
        sums = row(z).astype(F32)
        for term in arrived:
            sums = sums + term.astype(F32)
        owned, order = grating_blocks.shape[:2]
        reflected = jnp.concatenate(
            [
                lax.dot_general(
                    sums[:, b * order : (b + 1) * order],
                    grating_blocks[b],
                    LAST,
                    precision=lax.Precision.HIGHEST,
                )
                for b in range(owned)
            ],
            axis=1,
        ).astype(BF16)

        stack = jnp.zeros((z_count, rows, width), BF16)
        stack = lax.dynamic_update_slice(stack, reflected[None], (z, 0, 0))
        for dz in column:
            stack = lax.dynamic_update_slice(
                stack, flip(reflected, dz * y_count)[None], (z ^ dz, 0, 0)
            )
        waves = jnp.zeros(split, BF16)
        for dx, dy in [(0, 0)] + plane:
            piece = stack if (dx, dy) == (0, 0) else flip(stack, mask_of(dx, dy))
            waves = lax.dynamic_update_slice(
                waves, piece[:, None, None], (0, y ^ dy, x ^ dx, 0, 0)
            )
        mine = waves.reshape(blks, m // 2, width)
        other = flip(mine, core_mask)
        first = jnp.where(core == 0, mine, other)
        second = jnp.where(core == 0, other, mine)
        return jnp.concatenate([first, second], axis=1)

    up = [(i, i + 1) for i in range(devices - 1)]
    down = [(j, i) for i, j in up]
    first_index = me * count
    slots = (near_index - first_index + reach).astype(jnp.int32)
    incident_t = jnp.swapaxes(incident, 1, 2)
    other_part = (1 - core).astype(jnp.int32).reshape(1)
    own_part = core.astype(jnp.int32).reshape(1)

    high = solve(incident_t, t_matrices, reach, reach)
    low = solve(incident_t, t_matrices, 0, reach)
    for sweep in range(ITERS):
        send = outward(other_part, low, high, wave_basis, phases, 2, blks)
        keep = outward(own_part, low, high, wave_basis, phases, 2, blks)
        before = lax.ppermute(high, AXES, up)
        after = lax.ppermute(low, AXES, down)
        waves = reduce_reflect_gather(send, keep)
        partial = near(
            slots, near_count, near_type, before, low, high, after, incident_t, translations
        )
        if sweep == ITERS - 1:
            coeffs = back(phases, waves, wave_basis, partial, t_matrices, 0, count)
            return jnp.swapaxes(coeffs, 1, 2)
        high = back(phases, waves, wave_basis, partial, t_matrices, reach, reach)
        low = back(phases, waves, wave_basis, partial, t_matrices, 0, reach)


def solution(mesh):
    placed = (
        P(("dom", "blk"), None, None),
        P(("dom", "blk"), None, None),
        P(),
        P(("dom", "blk"), None),
        P(("dom", "blk")),
        P(("dom", "blk"), None),
        P(("dom", "blk"), None),
        P(),
        P("blk", None, None),
    )
    return jax.shard_map(
        local, mesh=mesh, in_specs=placed, out_specs=P(("dom", "blk"), None, None), check_vma=False
    )
```

```python
import jax
import jax.numpy as jnp
from jax import lax
from jax.experimental import pallas as pl
from jax.experimental.pallas import tpu as pltpu
from jax.sharding import PartitionSpec as P

ITERS = 2
AXES = ("dom", "blk")
F32 = jnp.float32
BF16 = jnp.bfloat16
LAST = (((1,), (1,)), ((), ()))
MIB = 1 << 20


def params(mib):
    return pltpu.CompilerParams(vmem_limit_bytes=mib * MIB)


def cost(macs, moved):
    return pl.CostEstimate(flops=1, bytes_accessed=1, transcendentals=0)


def solve_kernel(first_ref, source_ref, t_ref, out_ref, sources, matrices, arrived):
    count = out_ref.shape[0]
    copies = []
    for p in range(count):
        at = first_ref[0] * count + p
        pair = (
            pltpu.make_async_copy(source_ref.at[at], sources.at[p], arrived.at[2 * p]),
            pltpu.make_async_copy(t_ref.at[at], matrices.at[p], arrived.at[2 * p + 1]),
        )
        for copy in pair:
            copy.start()
        copies.append(pair)
    for p in range(count):
        for copy in copies[p]:
            copy.wait()
        out_ref[p] = lax.dot_general(
            sources[p], matrices[p], LAST, preferred_element_type=F32
        ).astype(BF16)


def solve(first, source, t_matrices, count):
    m, size = source.shape[1:]
    return pl.pallas_call(
        solve_kernel,
        grid_spec=pltpu.PrefetchScalarGridSpec(
            num_scalar_prefetch=1,
            grid=(1,),
            in_specs=[pl.BlockSpec(memory_space=pl.ANY)] * 2,
            out_specs=pl.BlockSpec((count, m, size), lambda p, first: (0, 0, 0)),
            scratch_shapes=[
                pltpu.VMEM((count, m, size), BF16),
                pltpu.VMEM((count, size, size), BF16),
                pltpu.SemaphoreType.DMA((2 * count,)),
            ],
        ),
        out_shape=jax.ShapeDtypeStruct((count, m, size), BF16),
        compiler_params=params(16),
        cost_estimate=cost(count * m * size * size, 2 * count * size * (2 * m + size)),
        name="solve",
    )(first, source, t_matrices)


def outward_kernel(part_ref, one_ref, two_ref, basis_ref, phase_ref, out_ref):
    half, rows, size = one_ref.shape
    chunks, _, chunk = out_ref.shape
    width = basis_ref.shape[0]
    total = jnp.zeros((rows, width), F32)
    for index, ref in ((0, one_ref), (half, two_ref)):
        spread = lax.dot_general(
            ref[...].reshape(half * rows, size),
            basis_ref[...],
            LAST,
            preferred_element_type=F32,
        )
        for p in range(half):
            phase = phase_ref[index + p, :].astype(F32)[None, :]
            total = total + phase * spread[p * rows : (p + 1) * rows]
    total = total.astype(BF16)
    for c in range(chunks):
        out_ref[c] = total[:, c * chunk : (c + 1) * chunk]


def outward(part, one, two, basis, phases, parts, chunks):
    half, m, size = one.shape
    total_rows = basis.shape[0]
    chunk = total_rows // chunks
    steps = 2
    width = total_rows // steps
    rows = m // parts
    return pl.pallas_call(
        outward_kernel,
        grid_spec=pltpu.PrefetchScalarGridSpec(
            num_scalar_prefetch=1,
            grid=(steps,),
            in_specs=[
                pl.BlockSpec((half, rows, size), lambda g, part: (0, part[0], 0)),
                pl.BlockSpec((half, rows, size), lambda g, part: (0, part[0], 0)),
                pl.BlockSpec((width, size), lambda g, part: (g, 0)),
                pl.BlockSpec((2 * half, width), lambda g, part: (0, g)),
            ],
            out_specs=pl.BlockSpec((chunks // steps, rows, chunk), lambda g, part: (g, 0, 0)),
        ),
        out_shape=jax.ShapeDtypeStruct((chunks, rows, chunk), BF16),
        compiler_params=params(24),
        cost_estimate=cost(
            2 * half * rows * size * total_rows, 2 * size * (total_rows + 2 * half * rows)
        ),
        name="outward",
    )(part, one, two, basis, phases)


def split_kernel(place_ref, offsets, levels, keep_ref, got_ref, *out_refs):
    across = keep_ref.shape[0] // levels
    for (dx, dy), out_ref in zip(offsets, out_refs):
        x, y = place_ref[0] ^ dx, place_ref[1] ^ dy
        for level in range(levels):
            chunk = level * across + y
            out_ref[level] = (
                keep_ref[chunk, x].astype(F32) + got_ref[chunk, x].astype(F32)
            ).astype(BF16)


def split(place, offsets, levels, keep, got):
    _, _, rows, width = keep.shape

    def body(place_ref, *refs):
        split_kernel(place_ref, offsets, levels, *refs)

    piece = jax.ShapeDtypeStruct((levels, rows, width), BF16)
    return pl.pallas_call(
        body,
        grid_spec=pltpu.PrefetchScalarGridSpec(
            num_scalar_prefetch=1,
            grid=(1,),
            in_specs=[pl.BlockSpec(keep.shape, lambda i, place: (0, 0, 0, 0))] * 2,
            out_specs=[pl.BlockSpec(piece.shape, lambda i, place: (0, 0, 0))] * len(offsets),
        ),
        out_shape=[piece] * len(offsets),
        compiler_params=params(8),
        cost_estimate=cost(keep.size, 6 * keep.size),
        name="split",
    )(place, keep, got)


def add_kernel(*refs):
    total = refs[0][...].astype(F32)
    for ref in refs[1:-1]:
        total = total + ref[...].astype(F32)
    refs[-1][...] = total.astype(BF16)


def add(*terms):
    return pl.pallas_call(
        add_kernel,
        out_shape=jax.ShapeDtypeStruct(terms[0].shape, BF16),
        compiler_params=params(8),
        cost_estimate=cost(len(terms) * terms[0].size, 2 * (len(terms) + 1) * terms[0].size),
        name="add",
    )(*terms)


def reflect_kernel(*refs):
    blocks_ref, out_ref = refs[-2:]
    levels, owned, order = blocks_ref.shape[:3]
    total = refs[0][...].astype(F32)
    for ref in refs[1:-2]:
        total = total + ref[...].astype(F32)
    total = total.astype(BF16)
    for level in range(levels):
        for b in range(owned):
            out_ref[level, :, b * order : (b + 1) * order] = lax.dot_general(
                total[level, :, b * order : (b + 1) * order],
                blocks_ref[level, b],
                LAST,
                preferred_element_type=F32,
            ).astype(BF16)


def reflect(terms, blocks):
    return pl.pallas_call(
        reflect_kernel,
        out_shape=jax.ShapeDtypeStruct(terms[0].shape, BF16),
        compiler_params=params(8),
        cost_estimate=cost(terms[0].size * 128, 2 * (len(terms) + 1) * terms[0].size),
        name="reflect",
    )(*terms, blocks)


def near_kernel(
    first_ref,
    slot_ref,
    count_ref,
    type_ref,
    halo_ref,
    own_ref,
    inner_ref,
    incident_ref,
    translations_ref,
    out_ref,
    extended,
    sums,
):
    group, m, size = incident_ref.shape
    kinds = translations_ref.shape[0]
    most = slot_ref.shape[1]
    for index, ref in enumerate((halo_ref, own_ref, inner_ref)):
        extended[pl.ds(index * group, group)] = ref[...]
    sums[...] = jnp.zeros(sums.shape, F32)
    for p in range(group):
        for k in range(most):

            @pl.when(k < count_ref[p])
            def _():
                place = type_ref[p, k]
                sums[place, p] += extended[slot_ref[p, k]].astype(F32)

    total = incident_ref[...].astype(F32).reshape(group * m, size)
    for t in range(kinds):
        total = total + lax.dot_general(
            sums[t].astype(BF16).reshape(group * m, size),
            translations_ref[t],
            LAST,
            preferred_element_type=F32,
        )
    out_ref[...] = total.reshape(group, m, size)


def near(first, slots, counts, types, halo, own, inner, incident, translations):
    m, size = incident.shape[1:]
    group = own.shape[0]
    kinds = translations.shape[0]
    whole = pl.BlockSpec((group, m, size), lambda p, *_: (0, 0, 0))
    return pl.pallas_call(
        near_kernel,
        grid_spec=pltpu.PrefetchScalarGridSpec(
            num_scalar_prefetch=4,
            grid=(1,),
            in_specs=[
                whole,
                whole,
                whole,
                pl.BlockSpec((group, m, size), lambda p, first, *_: (first[0], 0, 0)),
                pl.BlockSpec((kinds, size, size), lambda p, *_: (0, 0, 0)),
            ],
            out_specs=whole,
            scratch_shapes=[
                pltpu.VMEM((3 * group, m, size), BF16),
                pltpu.VMEM((kinds, group, m, size), F32),
            ],
        ),
        out_shape=jax.ShapeDtypeStruct((group, m, size), F32),
        compiler_params=params(32),
        cost_estimate=cost(kinds * group * m * size * size, 2 * size * size * kinds),
        name="near",
    )(first, slots, counts, types, halo, own, inner, incident, translations)


def back_kernel(first_ref, place_ref, offsets, refs):
    pieces = refs[: len(offsets)]
    phase_ref, basis_ref, partial_ref, t_ref = refs[len(offsets) : len(offsets) + 4]
    out_ref, waves = refs[-2:]
    group, m, size = partial_ref.shape
    chunks, parts, rows, width = waves.shape
    levels = pieces[0].shape[0]
    across = chunks // levels

    @pl.when(pl.program_id(0) == 0)
    def _():
        for (dc, dx, dy), piece in zip(offsets, pieces):
            part = (place_ref[2] ^ dc) * (parts // 2) + (place_ref[0] ^ dx)
            for level in range(levels):
                waves[level * across + (place_ref[1] ^ dy), part] = piece[level]

    total = partial_ref[...].reshape(group * m, size)
    for c in range(chunks):
        waves_here = waves[c].reshape(m, width)
        weighted = [
            phase_ref[i, :, pl.ds(c * width, width)] * waves_here for i in range(group)
        ]
        total = total + jnp.dot(
            jnp.concatenate(weighted, axis=0),
            basis_ref[pl.ds(c * width, width), :],
            preferred_element_type=F32,
        )
    source = total.astype(BF16)
    for i in range(group):
        out_ref[i] = lax.dot_general(
            source[i * m : (i + 1) * m], t_ref[i], LAST, preferred_element_type=F32
        ).astype(BF16)


def back(first, place, offsets, pieces, chunks, parts, phases, basis, partial, t_matrices, whole, onto=None):
    count, m, size = partial.shape
    levels, rows, width = pieces[0].shape
    total_rows = basis.shape[0]
    group = 2
    steps = count // group

    def body(first_ref, place_ref, *refs):
        if onto is not None:
            refs = refs[: len(offsets) + 4] + refs[len(offsets) + 5 :]
        back_kernel(first_ref, place_ref, offsets, refs)

    def here(p, first, place):
        return (first[0] * steps + p, 0, 0)

    def local_here(p, first, place):
        return (p, 0, 0)

    in_specs = [pl.BlockSpec((levels, rows, width), lambda p, *_: (0, 0, 0))] * len(pieces) + [
        pl.BlockSpec((group, 1, total_rows), here),
        pl.BlockSpec((total_rows, size), lambda p, *_: (0, 0)),
        pl.BlockSpec((group, m, size), local_here),
        pl.BlockSpec((group, size, size), here),
    ]
    operands = [first, place, *pieces, phases, basis, partial, t_matrices]
    aliases = {}
    if onto is not None:
        in_specs.append(pl.BlockSpec(memory_space=pl.ANY))
        aliases = {len(operands): 0}
        operands.append(onto)
    return pl.pallas_call(
        body,
        grid_spec=pltpu.PrefetchScalarGridSpec(
            num_scalar_prefetch=2,
            grid=(steps,),
            in_specs=in_specs,
            out_specs=pl.BlockSpec((group, m, size), here if whole else local_here),
            scratch_shapes=[pltpu.VMEM((chunks, parts, rows, width), BF16)],
        ),
        out_shape=jax.ShapeDtypeStruct((2 * count if whole else count, m, size), BF16),
        input_output_aliases=aliases,
        compiler_params=params(32),
        cost_estimate=cost(
            count * m * size * (total_rows + size), 2 * size * (total_rows + count * size)
        ),
        name="back",
    )(*operands)


def local(
    incident,
    t_matrices,
    translations,
    near_index,
    near_count,
    near_type,
    phases,
    wave_basis,
    grating_blocks,
):
    doms, blks = lax.axis_size("dom"), lax.axis_size("blk")
    devices = doms * blks
    levels = min(4, blks)
    y_count = blks // levels
    x_lo = min(2, doms // 2)
    x_hi = doms // 2 // x_lo
    count, size, m = incident.shape
    reach = count // 2
    me = lax.axis_index(AXES)
    dom, blk = lax.axis_index("dom"), lax.axis_index("blk")
    core, x = dom % 2, dom // 2 % x_lo
    z, y = blk // y_count, blk % y_count
    parts = 2 * x_lo
    rows = m // parts

    def flip(array, mask):
        return lax.ppermute(array, AXES, [(i, i ^ mask) for i in range(devices)])

    def scalar(*values):
        return jnp.stack([jnp.asarray(v, jnp.int32) for v in values])

    core_mask = blks
    plane = [(dx, dy) for dx in range(x_lo) for dy in range(y_count) if (dx, dy) != (0, 0)]
    plane.sort(key=lambda pair: -(pair[0] > 0) - (pair[1] > 0))
    plane_masks = [dx * 2 * blks + dy for dx, dy in plane]
    offsets = [(0, 0)] + plane
    all_offsets = [(dc, dx, dy) for dc in (0, 1) for dx, dy in offsets]
    columns = [
        (h, d) for h in range(x_hi) for d in (2, 3, 1, 0) if d < levels and (h, d) != (0, 0)
    ]
    column_masks = [h * x_lo * 2 * blks + d * y_count for h, d in columns]
    place = scalar(x, y, core)

    even = me % 2 == 0
    e_group = jnp.where(even, 1, 0).astype(jnp.int32)
    o_group = 1 - e_group
    e_pairs = [(i, i ^ 1) for i in range(devices)]
    o_pairs = [(i, i - 1 if i % 2 == 0 else i + 1) for i in range(1, devices - 1)]
    side = (near_index - me * count + reach) // reach
    within = (near_index - me * count + reach) % reach

    def lists(group):
        def taken(array):
            return lax.dynamic_slice_in_dim(array, group * reach, reach, axis=0)

        position = jnp.where(group == 0, side, 3 - side)
        slots = jnp.clip(position * reach + within, 0, 3 * reach - 1)
        return taken(slots).astype(jnp.int32), taken(near_count), taken(near_type)

    e_lists, o_lists = lists(e_group), lists(o_group)
    e_first, o_first = scalar(e_group), scalar(o_group)
    incident_t = jnp.swapaxes(incident, 1, 2)
    phase_rows = phases[:, None, :]
    grouped_phases = jnp.concatenate(
        [lax.dynamic_slice_in_dim(phases, g * reach, reach, axis=0) for g in (o_group, e_group)],
        axis=0,
    )

    held = [pltpu.with_memory_space_constraint(a, pltpu.HBM) for a in (incident_t, t_matrices)]
    o_coeffs = solve(o_first, *held, reach)
    e_coeffs = solve(e_first, *held, reach)
    for sweep in range(ITERS):
        o_halo = lax.ppermute(o_coeffs, AXES, o_pairs)
        send = outward(
            scalar(1 - core), o_coeffs, e_coeffs, wave_basis, grouped_phases, 2, blks
        )
        got = flip(send, core_mask)
        keep = outward(scalar(core), o_coeffs, e_coeffs, wave_basis, grouped_phases, 2, blks)
        shape = (blks, x_lo, rows, keep.shape[2])
        pieces = split(place, offsets, levels, keep.reshape(shape), got.reshape(shape))
        arrived = [flip(piece, mask) for piece, mask in zip(pieces[1:], plane_masks)]
        if sweep == 0:
            own_blocks, _ = lax.optimization_barrier((grating_blocks.astype(BF16), pieces[0]))
            gathered = jnp.zeros((levels,) + own_blocks.shape, BF16)
            gathered = lax.dynamic_update_slice(gathered, own_blocks[None], (z, 0, 0, 0))
            for d in range(1, levels):
                gathered = lax.dynamic_update_slice(
                    gathered, flip(own_blocks, d * y_count)[None], (z ^ d, 0, 0, 0)
                )
        arrived, o_halo = lax.optimization_barrier((arrived, o_halo))
        plane_sum = add(pieces[0], *arrived)
        e_sent, _ = lax.optimization_barrier((e_coeffs, plane_sum))
        e_halo = lax.ppermute(e_sent, AXES, e_pairs)
        o_near = near(
            o_first, *o_lists, o_halo, o_coeffs, e_coeffs, incident_t, translations
        )
        arrived = [flip(plane_sum, mask) for mask in column_masks]
        arrived, o_near = lax.optimization_barrier((arrived, o_near))
        stack = reflect([plane_sum, *arrived], gathered)
        e_near = near(
            e_first, *e_lists, e_halo, e_coeffs, o_coeffs, incident_t, translations
        )
        stacks = [stack] + [flip(stack, mask) for mask in plane_masks]
        late = [n for n, (dx, dy) in enumerate(offsets) if dy]
        held, e_near = lax.optimization_barrier(([stacks[n] for n in late], e_near))
        for n, piece in zip(late, held):
            stacks[n] = piece
        stacks = stacks + [flip(piece, core_mask) for piece in stacks]
        last = sweep == ITERS - 1
        common = (place, all_offsets, stacks, blks, parts, phase_rows, wave_basis)
        o_coeffs = back(o_first, *common, o_near, t_matrices, last)
        if not last:
            e_near, _ = lax.optimization_barrier((e_near, o_coeffs))
        e_coeffs = back(
            e_first, *common, e_near, t_matrices, last, o_coeffs if last else None
        )
    return jnp.swapaxes(e_coeffs, 1, 2)


def solution(mesh):
    placed = (
        P(("dom", "blk"), None, None),
        P(("dom", "blk"), None, None),
        P(),
        P(("dom", "blk"), None),
        P(("dom", "blk")),
        P(("dom", "blk"), None),
        P(("dom", "blk"), None),
        P(),
        P("blk", None, None),
    )
    return jax.shard_map(
        local, mesh=mesh, in_specs=placed, out_specs=P(("dom", "blk"), None, None), check_vma=False
    )
```

```python
import jax
import jax.numpy as jnp
from jax import lax
from jax.experimental import pallas as pl
from jax.experimental.pallas import tpu as pltpu
from jax.sharding import PartitionSpec as P

ITERS = 2
AXES = ("dom", "blk")
F32 = jnp.float32
BF16 = jnp.bfloat16
LAST = (((1,), (1,)), ((), ()))
MIB = 1 << 20


SCALARS = pl.BlockSpec(memory_space=pltpu.SMEM)
VECTORS = pl.BlockSpec(memory_space=pltpu.VMEM)


def params(mib):
    return pltpu.CompilerParams(vmem_limit_bytes=mib * MIB)


def cost(macs, moved):
    return pl.CostEstimate(flops=1, bytes_accessed=1, transcendentals=0)


def solve_kernel(first_ref, source_ref, t_ref, out_ref, sources, matrices, arrived):
    count = out_ref.shape[0]
    copies = []
    for p in range(count):
        at = first_ref[0] * count + p
        pair = (
            pltpu.make_async_copy(source_ref.at[at], sources.at[p], arrived.at[2 * p]),
            pltpu.make_async_copy(t_ref.at[at], matrices.at[p], arrived.at[2 * p + 1]),
        )
        for copy in pair:
            copy.start()
        copies.append(pair)
    for p in range(count):
        for copy in copies[p]:
            copy.wait()
        out_ref[p] = lax.dot_general(
            sources[p], matrices[p], LAST, preferred_element_type=F32
        ).astype(BF16)


def solve(first, source, t_matrices, count):
    m, size = source.shape[1:]
    return pl.pallas_call(
        solve_kernel,
        grid_spec=pltpu.PrefetchScalarGridSpec(
            num_scalar_prefetch=1,
            grid=(1,),
            in_specs=[pl.BlockSpec(memory_space=pl.ANY)] * 2,
            out_specs=pl.BlockSpec((count, m, size), lambda p, first: (0, 0, 0)),
            scratch_shapes=[
                pltpu.VMEM((count, m, size), BF16),
                pltpu.VMEM((count, size, size), BF16),
                pltpu.SemaphoreType.DMA((2 * count,)),
            ],
        ),
        out_shape=jax.ShapeDtypeStruct((count, m, size), BF16),
        compiler_params=params(16),
        cost_estimate=cost(count * m * size * size, 2 * count * size * (2 * m + size)),
        name="solve",
    )(first, source, t_matrices)


def outward_kernel(part_ref, one_ref, two_ref, basis_ref, phase_ref, out_ref):
    half, rows, size = one_ref.shape
    chunks, _, chunk = out_ref.shape
    width = basis_ref.shape[0]
    total = jnp.zeros((rows, width), F32)
    for index, ref in ((0, one_ref), (half, two_ref)):
        spread = lax.dot_general(
            ref[...].reshape(half * rows, size),
            basis_ref[...],
            LAST,
            preferred_element_type=F32,
        )
        for p in range(half):
            phase = phase_ref[index + p, :].astype(F32)[None, :]
            total = total + phase * spread[p * rows : (p + 1) * rows]
    total = total.astype(BF16)
    for c in range(chunks):
        out_ref[c] = total[:, c * chunk : (c + 1) * chunk]


def outward(part, one, two, basis, phases, parts, chunks):
    half, m, size = one.shape
    total_rows = basis.shape[0]
    chunk = total_rows // chunks
    steps = 2
    width = total_rows // steps
    rows = m // parts
    return pl.pallas_call(
        outward_kernel,
        grid_spec=pltpu.PrefetchScalarGridSpec(
            num_scalar_prefetch=1,
            grid=(steps,),
            in_specs=[
                pl.BlockSpec((half, rows, size), lambda g, part: (0, part[0], 0)),
                pl.BlockSpec((half, rows, size), lambda g, part: (0, part[0], 0)),
                pl.BlockSpec((width, size), lambda g, part: (g, 0)),
                pl.BlockSpec((2 * half, width), lambda g, part: (0, g)),
            ],
            out_specs=pl.BlockSpec((chunks // steps, rows, chunk), lambda g, part: (g, 0, 0)),
        ),
        out_shape=jax.ShapeDtypeStruct((chunks, rows, chunk), BF16),
        compiler_params=params(24),
        cost_estimate=cost(
            2 * half * rows * size * total_rows, 2 * size * (total_rows + 2 * half * rows)
        ),
        name="outward",
    )(part, one, two, basis, phases)


def split_kernel(place_ref, keep_ref, got_ref, here_ref, there_ref):
    for dx, out_ref in ((0, here_ref), (1, there_ref)):
        x = place_ref[0] ^ dx
        for chunk in range(keep_ref.shape[0]):
            out_ref[chunk] = (
                keep_ref[chunk, x].astype(F32) + got_ref[chunk, x].astype(F32)
            ).astype(BF16)


def split(place, keep, got):
    chunks, _, rows, width = keep.shape
    return pl.pallas_call(
        split_kernel,
        in_specs=[SCALARS, VECTORS, VECTORS],
        out_specs=[VECTORS] * 2,
        out_shape=[jax.ShapeDtypeStruct((chunks, rows, width), BF16)] * 2,
        compiler_params=params(4),
        cost_estimate=cost(keep.size, 6 * keep.size),
        name="split",
    )(place, keep, got)


def deal_kernel(place_ref, mine_ref, got_ref, *out_refs):
    levels = out_refs[0].shape[0]
    across = mine_ref.shape[0] // levels
    for dy, out_ref in enumerate(out_refs):
        for level in range(levels):
            chunk = level * across + (place_ref[1] ^ dy)
            out_ref[level] = (
                mine_ref[chunk].astype(F32) + got_ref[chunk].astype(F32)
            ).astype(BF16)


def deal(place, levels, mine, got):
    chunks, rows, width = mine.shape
    across = chunks // levels
    return pl.pallas_call(
        deal_kernel,
        in_specs=[SCALARS, VECTORS, VECTORS],
        out_specs=[VECTORS] * across,
        out_shape=[jax.ShapeDtypeStruct((levels, rows, width), BF16)] * across,
        compiler_params=params(4),
        cost_estimate=cost(mine.size, 6 * mine.size),
        name="deal",
    )(place, mine, got)


def add_kernel(*refs):
    total = refs[0][...].astype(F32)
    for ref in refs[1:-1]:
        total = total + ref[...].astype(F32)
    refs[-1][...] = total.astype(BF16)


def add(*terms):
    return pl.pallas_call(
        add_kernel,
        out_shape=jax.ShapeDtypeStruct(terms[0].shape, BF16),
        compiler_params=params(8),
        cost_estimate=cost(len(terms) * terms[0].size, 2 * (len(terms) + 1) * terms[0].size),
        name="add",
    )(*terms)


def reflect_kernel(*refs):
    blocks_ref, out_ref = refs[-2:]
    levels, owned, order = blocks_ref.shape[:3]
    total = refs[0][...].astype(F32)
    for ref in refs[1:-2]:
        total = total + ref[...].astype(F32)
    total = total.astype(BF16)
    for level in range(levels):
        for b in range(owned):
            out_ref[level, :, b * order : (b + 1) * order] = lax.dot_general(
                total[level, :, b * order : (b + 1) * order],
                blocks_ref[level, b],
                LAST,
                preferred_element_type=F32,
            ).astype(BF16)


def reflect(terms, blocks):
    return pl.pallas_call(
        reflect_kernel,
        out_shape=jax.ShapeDtypeStruct(terms[0].shape, BF16),
        compiler_params=params(8),
        cost_estimate=cost(terms[0].size * 128, 2 * (len(terms) + 1) * terms[0].size),
        name="reflect",
    )(*terms, blocks)


def near_kernel(
    first_ref,
    slot_ref,
    count_ref,
    type_ref,
    halo_ref,
    own_ref,
    inner_ref,
    incident_ref,
    translations_ref,
    out_ref,
    extended,
    sums,
):
    group, m, size = incident_ref.shape
    kinds = translations_ref.shape[0]
    most = slot_ref.shape[1]
    for index, ref in enumerate((halo_ref, own_ref, inner_ref)):
        extended[pl.ds(index * group, group)] = ref[...]
    sums[...] = jnp.zeros(sums.shape, F32)
    for p in range(group):
        for k in range(most):

            @pl.when(k < count_ref[p])
            def _():
                place = type_ref[p, k]
                sums[place, p] += extended[slot_ref[p, k]].astype(F32)

    total = incident_ref[...].astype(F32).reshape(group * m, size)
    for t in range(kinds):
        total = total + lax.dot_general(
            sums[t].astype(BF16).reshape(group * m, size),
            translations_ref[t],
            LAST,
            preferred_element_type=F32,
        )
    out_ref[...] = total.reshape(group, m, size)


def near(first, slots, counts, types, halo, own, inner, incident, translations):
    m, size = incident.shape[1:]
    group = own.shape[0]
    kinds = translations.shape[0]
    whole = pl.BlockSpec((group, m, size), lambda p, *_: (0, 0, 0))
    return pl.pallas_call(
        near_kernel,
        grid_spec=pltpu.PrefetchScalarGridSpec(
            num_scalar_prefetch=4,
            grid=(1,),
            in_specs=[
                whole,
                whole,
                whole,
                pl.BlockSpec((group, m, size), lambda p, first, *_: (first[0], 0, 0)),
                pl.BlockSpec((kinds, size, size), lambda p, *_: (0, 0, 0)),
            ],
            out_specs=whole,
            scratch_shapes=[
                pltpu.VMEM((3 * group, m, size), BF16),
                pltpu.VMEM((kinds, group, m, size), F32),
            ],
        ),
        out_shape=jax.ShapeDtypeStruct((group, m, size), F32),
        compiler_params=params(32),
        cost_estimate=cost(kinds * group * m * size * size, 2 * size * size * kinds),
        name="near",
    )(first, slots, counts, types, halo, own, inner, incident, translations)


def back_kernel(first_ref, place_ref, offsets, refs):
    pieces = refs[: len(offsets)]
    phase_ref, basis_ref, partial_ref, t_ref = refs[len(offsets) : len(offsets) + 4]
    out_ref, waves = refs[-2:]
    group, m, size = partial_ref.shape
    chunks, parts, rows, width = waves.shape
    levels = pieces[0].shape[0]
    across = chunks // levels

    @pl.when(pl.program_id(0) == 0)
    def _():
        for (dc, dx, dy), piece in zip(offsets, pieces):
            part = (place_ref[2] ^ dc) * (parts // 2) + (place_ref[0] ^ dx)
            for level in range(levels):
                waves[level * across + (place_ref[1] ^ dy), part] = piece[level]

    total = partial_ref[...].reshape(group * m, size)
    for c in range(chunks):
        waves_here = waves[c].reshape(m, width)
        weighted = [
            phase_ref[i, :, pl.ds(c * width, width)] * waves_here for i in range(group)
        ]
        total = total + jnp.dot(
            jnp.concatenate(weighted, axis=0),
            basis_ref[pl.ds(c * width, width), :],
            preferred_element_type=F32,
        )
    source = total.astype(BF16)
    for i in range(group):
        out_ref[i] = lax.dot_general(
            source[i * m : (i + 1) * m], t_ref[i], LAST, preferred_element_type=F32
        ).astype(BF16)


def back(first, place, offsets, pieces, chunks, parts, phases, basis, partial, t_matrices, whole, onto=None):
    count, m, size = partial.shape
    levels, rows, width = pieces[0].shape
    total_rows = basis.shape[0]
    group = 2
    steps = count // group

    def body(first_ref, place_ref, *refs):
        if onto is not None:
            refs = refs[: len(offsets) + 4] + refs[len(offsets) + 5 :]
        back_kernel(first_ref, place_ref, offsets, refs)

    def here(p, first, place):
        return (first[0] * steps + p, 0, 0)

    def local_here(p, first, place):
        return (p, 0, 0)

    in_specs = [pl.BlockSpec((levels, rows, width), lambda p, *_: (0, 0, 0))] * len(pieces) + [
        pl.BlockSpec((group, 1, total_rows), here),
        pl.BlockSpec((total_rows, size), lambda p, *_: (0, 0)),
        pl.BlockSpec((group, m, size), local_here),
        pl.BlockSpec((group, size, size), here),
    ]
    operands = [first, place, *pieces, phases, basis, partial, t_matrices]
    aliases = {}
    if onto is not None:
        in_specs.append(pl.BlockSpec(memory_space=pl.ANY))
        aliases = {len(operands): 0}
        operands.append(onto)
    return pl.pallas_call(
        body,
        grid_spec=pltpu.PrefetchScalarGridSpec(
            num_scalar_prefetch=2,
            grid=(steps,),
            in_specs=in_specs,
            out_specs=pl.BlockSpec((group, m, size), here if whole else local_here),
            scratch_shapes=[pltpu.VMEM((chunks, parts, rows, width), BF16)],
        ),
        out_shape=jax.ShapeDtypeStruct((2 * count if whole else count, m, size), BF16),
        input_output_aliases=aliases,
        compiler_params=params(32),
        cost_estimate=cost(
            count * m * size * (total_rows + size), 2 * size * (total_rows + count * size)
        ),
        name="back",
    )(*operands)


def local(
    incident,
    t_matrices,
    translations,
    near_index,
    near_count,
    near_type,
    phases,
    wave_basis,
    grating_blocks,
):
    doms, blks = lax.axis_size("dom"), lax.axis_size("blk")
    devices = doms * blks
    levels = min(4, blks)
    y_count = blks // levels
    x_lo = min(2, doms // 2)
    x_hi = doms // 2 // x_lo
    count, size, m = incident.shape
    reach = count // 2
    me = lax.axis_index(AXES)
    dom, blk = lax.axis_index("dom"), lax.axis_index("blk")
    core, x = dom % 2, dom // 2 % x_lo
    z, y = blk // y_count, blk % y_count
    parts = 2 * x_lo
    rows = m // parts

    def flip(array, mask):
        return lax.ppermute(array, AXES, [(i, i ^ mask) for i in range(devices)])

    def scalar(*values):
        return jnp.stack([jnp.asarray(v, jnp.int32) for v in values])

    core_mask, x_mask = blks, 2 * blks
    turns = [bin(dy).count("1") % 2 for dy in range(y_count)]
    y_masks = [turn * x_mask + dy for dy, turn in enumerate(turns)]
    twist = sum(jnp.where(y == dy, turn, 0) for dy, turn in enumerate(turns))
    offsets = [(dh, dy) for dh in (0, 1) for dy in range(y_count)]
    all_offsets = [(dc, dh, dy) for dc in (0, 1) for dh, dy in offsets]
    columns = [
        (h, d) for h in range(x_hi) for d in (2, 3, 1, 0) if d < levels and (h, d) != (0, 0)
    ]
    column_masks = [h * x_lo * 2 * blks + d * y_count for h, d in columns]
    place = scalar(x ^ twist, y, core)

    even = me % 2 == 0
    e_group = jnp.where(even, 1, 0).astype(jnp.int32)
    o_group = 1 - e_group
    e_pairs = [(i, i ^ 1) for i in range(devices)]
    o_pairs = [(i, i - 1 if i % 2 == 0 else i + 1) for i in range(1, devices - 1)]
    side = (near_index - me * count + reach) // reach
    within = (near_index - me * count + reach) % reach

    def lists(group):
        def taken(array):
            return lax.dynamic_slice_in_dim(array, group * reach, reach, axis=0)

        position = jnp.where(group == 0, side, 3 - side)
        slots = jnp.clip(position * reach + within, 0, 3 * reach - 1)
        return taken(slots).astype(jnp.int32), taken(near_count), taken(near_type)

    e_lists, o_lists = lists(e_group), lists(o_group)
    e_first, o_first = scalar(e_group), scalar(o_group)
    incident_t = jnp.swapaxes(incident, 1, 2)
    phase_rows = phases[:, None, :]
    grouped_phases = jnp.concatenate(
        [lax.dynamic_slice_in_dim(phases, g * reach, reach, axis=0) for g in (o_group, e_group)],
        axis=0,
    )

    held = [pltpu.with_memory_space_constraint(a, pltpu.HBM) for a in (incident_t, t_matrices)]
    o_coeffs = solve(o_first, *held, reach)
    e_coeffs = solve(e_first, *held, reach)
    for sweep in range(ITERS):
        o_halo = lax.ppermute(o_coeffs, AXES, o_pairs)
        send = outward(
            scalar(1 - core), o_coeffs, e_coeffs, wave_basis, grouped_phases, 2, blks
        )
        got = flip(send, core_mask)
        keep = outward(scalar(core), o_coeffs, e_coeffs, wave_basis, grouped_phases, 2, blks)
        shape = (blks, x_lo, rows, keep.shape[2])
        mine, theirs = split(place, keep.reshape(shape), got.reshape(shape))
        pieces = deal(place, levels, mine, flip(theirs, x_mask))
        arrived = [flip(pieces[dy], y_masks[dy]) for dy in range(1, y_count)]
        if sweep == 0:
            own_blocks, _ = lax.optimization_barrier((grating_blocks.astype(BF16), mine))
            gathered = jnp.zeros((levels,) + own_blocks.shape, BF16)
            gathered = lax.dynamic_update_slice(gathered, own_blocks[None], (z, 0, 0, 0))
            for d in range(1, levels):
                gathered = lax.dynamic_update_slice(
                    gathered, flip(own_blocks, d * y_count)[None], (z ^ d, 0, 0, 0)
                )
        arrived, o_halo = lax.optimization_barrier((arrived, o_halo))
        plane_sum = add(pieces[0], *arrived)
        e_sent, _ = lax.optimization_barrier((e_coeffs, plane_sum))
        e_halo = lax.ppermute(e_sent, AXES, e_pairs)
        o_near = near(
            o_first, *o_lists, o_halo, o_coeffs, e_coeffs, incident_t, translations
        )
        arrived = [flip(plane_sum, mask) for mask in column_masks]
        arrived, o_near = lax.optimization_barrier((arrived, o_near))
        stack = reflect([plane_sum, *arrived], gathered)
        e_near = near(
            e_first, *e_lists, e_halo, e_coeffs, o_coeffs, incident_t, translations
        )
        stacks = [stack] + [flip(stack, mask) for mask in y_masks[1:]]
        stacks = stacks + [flip(piece, x_mask) for piece in stacks]
        late = [n for n, (dh, dy) in enumerate(offsets) if dh and dy]
        held, e_near = lax.optimization_barrier(([stacks[n] for n in late], e_near))
        for n, piece in zip(late, held):
            stacks[n] = piece
        stacks = stacks + [flip(piece, core_mask) for piece in stacks]
        last = sweep == ITERS - 1
        common = (place, all_offsets, stacks, blks, parts, phase_rows, wave_basis)
        o_coeffs = back(o_first, *common, o_near, t_matrices, last)
        if not last:
            e_near, _ = lax.optimization_barrier((e_near, o_coeffs))
        e_coeffs = back(
            e_first, *common, e_near, t_matrices, last, o_coeffs if last else None
        )
    return jnp.swapaxes(e_coeffs, 1, 2)


def solution(mesh):
    placed = (
        P(("dom", "blk"), None, None),
        P(("dom", "blk"), None, None),
        P(),
        P(("dom", "blk"), None),
        P(("dom", "blk")),
        P(("dom", "blk"), None),
        P(("dom", "blk"), None),
        P(),
        P("blk", None, None),
    )
    return jax.shard_map(
        local, mesh=mesh, in_specs=placed, out_specs=P(("dom", "blk"), None, None), check_vma=False
    )
```

```python
import jax
import jax.numpy as jnp
from jax import lax
from jax.experimental import pallas as pl
from jax.experimental.pallas import tpu as pltpu
from jax.sharding import PartitionSpec as P

ITERS = 2
AXES = ("dom", "blk")
F32 = jnp.float32
BF16 = jnp.bfloat16
LAST = (((1,), (1,)), ((), ()))
MIB = 1 << 20


SCALARS = pl.BlockSpec(memory_space=pltpu.SMEM)
VECTORS = pl.BlockSpec(memory_space=pltpu.VMEM)
ANYWHERE = pl.BlockSpec(memory_space=pl.ANY)


def params(mib):
    return pltpu.CompilerParams(vmem_limit_bytes=mib * MIB)


def cost(macs, moved, real=False):
    if real:
        return pl.CostEstimate(flops=2 * macs, bytes_accessed=moved, transcendentals=0)
    return pl.CostEstimate(flops=1, bytes_accessed=1, transcendentals=0)


def solve_kernel(first_ref, source_ref, t_ref, out_ref, sources, matrices, arrived):
    count = out_ref.shape[0]
    copies = []
    for p in range(count):
        at = first_ref[0] * count + p
        pair = (
            pltpu.make_async_copy(source_ref.at[at], sources.at[p], arrived.at[2 * p]),
            pltpu.make_async_copy(t_ref.at[at], matrices.at[p], arrived.at[2 * p + 1]),
        )
        for copy in pair:
            copy.start()
        copies.append(pair)
    for p in range(count):
        for copy in copies[p]:
            copy.wait()
        out_ref[p] = lax.dot_general(
            sources[p], matrices[p], LAST, preferred_element_type=F32
        ).astype(BF16)


def solve(first, source, t_matrices, count):
    m, size = source.shape[1:]
    return pl.pallas_call(
        solve_kernel,
        grid_spec=pltpu.PrefetchScalarGridSpec(
            num_scalar_prefetch=1,
            grid=(1,),
            in_specs=[pl.BlockSpec(memory_space=pl.ANY)] * 2,
            out_specs=pl.BlockSpec((count, m, size), lambda p, first: (0, 0, 0)),
            scratch_shapes=[
                pltpu.VMEM((count, m, size), BF16),
                pltpu.VMEM((count, size, size), BF16),
                pltpu.SemaphoreType.DMA((2 * count,)),
            ],
        ),
        out_shape=jax.ShapeDtypeStruct((count, m, size), BF16),
        compiler_params=params(16),
        cost_estimate=cost(count * m * size * size, 2 * count * size * (2 * m + size)),
        name="solve",
    )(first, source, t_matrices)


def outward_kernel(part_ref, *refs):
    pieces, (basis_ref, phase_ref, out_ref) = refs[:-3], refs[-3:]
    chunks, rows, chunk = out_ref.shape
    total_rows, size = basis_ref.shape
    width = min(1024, total_rows)
    start = pl.multiple_of(part_ref[0] * rows, 16)
    source = jnp.concatenate(
        [ref[:, pl.ds(start, rows), :].reshape(-1, size) for ref in pieces], axis=0
    )
    for g in range(0, total_rows, width):
        spread = lax.dot_general(
            source, basis_ref[g : g + width, :], LAST, preferred_element_type=F32
        )
        total = phase_ref[0:1, g : g + width] * spread[:rows]
        for p in range(1, phase_ref.shape[0]):
            total = total + phase_ref[p : p + 1, g : g + width] * spread[p * rows : (p + 1) * rows]
        total = total.astype(BF16)
        for c in range(0, width, chunk):
            out_ref[(g + c) // chunk] = total[:, c : c + chunk]


def outward(part, pieces, basis, phases, parts, chunks):
    m, size = pieces[0].shape[1:]
    count, total_rows = phases.shape
    chunk = total_rows // chunks
    rows = m // parts
    return pl.pallas_call(
        outward_kernel,
        in_specs=[SCALARS] + [VECTORS] * (len(pieces) + 2),
        out_specs=VECTORS,
        out_shape=jax.ShapeDtypeStruct((chunks, rows, chunk), BF16),
        compiler_params=params(16),
        cost_estimate=cost(count * rows * size * total_rows, 2 * size * total_rows),
        name="outward",
    )(part, *pieces, basis, phases)


def split_kernel(place_ref, keep_ref, got_ref, here_ref, there_ref):
    for dx, out_ref in ((0, here_ref), (1, there_ref)):
        x = place_ref[0] ^ dx
        for chunk in range(keep_ref.shape[0]):
            out_ref[chunk] = (
                keep_ref[chunk, x].astype(F32) + got_ref[chunk, x].astype(F32)
            ).astype(BF16)


def split(place, keep, got):
    chunks, _, rows, width = keep.shape
    return pl.pallas_call(
        split_kernel,
        in_specs=[SCALARS, VECTORS, VECTORS],
        out_specs=[VECTORS] * 2,
        out_shape=[jax.ShapeDtypeStruct((chunks, rows, width), BF16)] * 2,
        compiler_params=params(4),
        cost_estimate=cost(keep.size, 6 * keep.size),
        name="split",
    )(place, keep, got)


def deal_kernel(place_ref, mine_ref, got_ref, *out_refs):
    levels = out_refs[0].shape[0]
    across = mine_ref.shape[0] // levels
    for dy, out_ref in enumerate(out_refs):
        for level in range(levels):
            chunk = level * across + (place_ref[1] ^ dy)
            out_ref[level] = (
                mine_ref[chunk].astype(F32) + got_ref[chunk].astype(F32)
            ).astype(BF16)


def deal(place, levels, mine, got):
    chunks, rows, width = mine.shape
    across = chunks // levels
    return pl.pallas_call(
        deal_kernel,
        in_specs=[SCALARS, VECTORS, VECTORS],
        out_specs=[VECTORS] * across,
        out_shape=[jax.ShapeDtypeStruct((levels, rows, width), BF16)] * across,
        compiler_params=params(4),
        cost_estimate=cost(mine.size, 6 * mine.size),
        name="deal",
    )(place, mine, got)


def add_kernel(*refs):
    total = refs[0][...].astype(F32)
    for ref in refs[1:-1]:
        total = total + ref[...].astype(F32)
    refs[-1][...] = total.astype(BF16)


def add(*terms):
    return pl.pallas_call(
        add_kernel,
        out_shape=jax.ShapeDtypeStruct(terms[0].shape, BF16),
        compiler_params=params(8),
        cost_estimate=cost(len(terms) * terms[0].size, 2 * (len(terms) + 1) * terms[0].size),
        name="add",
    )(*terms)


def reflect_kernel(*refs):
    blocks_ref, out_ref = refs[-2:]
    levels, owned, order = blocks_ref.shape[:3]
    total = refs[0][...].astype(F32)
    for ref in refs[1:-2]:
        total = total + ref[...].astype(F32)
    total = total.astype(BF16)
    for level in range(levels):
        for b in range(owned):
            out_ref[level, :, b * order : (b + 1) * order] = lax.dot_general(
                total[level, :, b * order : (b + 1) * order],
                blocks_ref[level, b],
                LAST,
                preferred_element_type=F32,
            ).astype(BF16)


def reflect(terms, blocks):
    return pl.pallas_call(
        reflect_kernel,
        out_shape=jax.ShapeDtypeStruct(terms[0].shape, BF16),
        compiler_params=params(8),
        cost_estimate=cost(terms[0].size * 128, 2 * (len(terms) + 1) * terms[0].size),
        name="reflect",
    )(*terms, blocks)


def near_kernel(
    first_ref,
    slot_ref,
    count_ref,
    type_ref,
    halo_ref,
    own_ref,
    inner_ref,
    incident_ref,
    translations_ref,
    out_ref,
    extended,
    sums,
):
    group, m, size = incident_ref.shape
    kinds = translations_ref.shape[0]
    most = slot_ref.shape[1]
    for index, ref in enumerate((halo_ref, own_ref, inner_ref)):
        extended[pl.ds(index * group, group)] = ref[...]
    sums[...] = jnp.zeros(sums.shape, F32)
    for p in range(group):
        for k in range(most):

            @pl.when(k < count_ref[p])
            def _():
                place = type_ref[p, k]
                sums[place, p] += extended[slot_ref[p, k]].astype(F32)

    total = incident_ref[...].astype(F32).reshape(group * m, size)
    for t in range(kinds):
        total = total + lax.dot_general(
            sums[t].astype(BF16).reshape(group * m, size),
            translations_ref[t],
            LAST,
            preferred_element_type=F32,
        )
    out_ref[...] = total.reshape(group, m, size)


def near(first, slots, counts, types, halo, own, inner, incident, translations):
    m, size = incident.shape[1:]
    group = own.shape[0]
    kinds = translations.shape[0]
    whole = pl.BlockSpec((group, m, size), lambda p, *_: (0, 0, 0))
    return pl.pallas_call(
        near_kernel,
        grid_spec=pltpu.PrefetchScalarGridSpec(
            num_scalar_prefetch=4,
            grid=(1,),
            in_specs=[
                whole,
                whole,
                whole,
                pl.BlockSpec((group, m, size), lambda p, first, *_: (first[0], 0, 0)),
                pl.BlockSpec((kinds, size, size), lambda p, *_: (0, 0, 0)),
            ],
            out_specs=whole,
            scratch_shapes=[
                pltpu.VMEM((3 * group, m, size), BF16),
                pltpu.VMEM((kinds, group, m, size), F32),
            ],
        ),
        out_shape=jax.ShapeDtypeStruct((group, m, size), F32),
        compiler_params=params(32),
        cost_estimate=cost(kinds * group * m * size * size, 2 * size * size * kinds),
        name="near",
    )(first, slots, counts, types, halo, own, inner, incident, translations)


def back_kernel(first_ref, place_ref, offsets, refs):
    pieces = refs[: len(offsets)]
    phase_ref, basis_ref, t_ref = refs[len(offsets) : len(offsets) + 3]
    partials = refs[len(offsets) + 3 : -2]
    out_ref, waves = refs[-2:]
    group, m, size = out_ref.shape
    chunks, parts, rows, width = waves.shape
    levels = pieces[0].shape[0]
    across = chunks // levels

    @pl.when(pl.program_id(0) == 0)
    def _():
        for (dc, dx, dy), piece in zip(offsets, pieces):
            part = (place_ref[2] ^ dc) * (parts // 2) + (place_ref[0] ^ dx)
            for level in range(levels):
                waves[level * across + (place_ref[1] ^ dy), part] = piece[level]

    total = partials[0][...]
    if len(partials) > 1:
        total = jnp.where(pl.program_id(0) // 2 == first_ref[0], total, partials[1][...])
    total = total.reshape(group * m, size)
    for c in range(chunks):
        waves_here = waves[c].reshape(m, width)
        weighted = [
            phase_ref[i, :, pl.ds(c * width, width)] * waves_here for i in range(group)
        ]
        total = total + jnp.dot(
            jnp.concatenate(weighted, axis=0),
            basis_ref[pl.ds(c * width, width), :],
            preferred_element_type=F32,
        )
    source = total.astype(BF16)
    for i in range(group):
        out_ref[i] = lax.dot_general(
            source[i * m : (i + 1) * m], t_ref[i], LAST, preferred_element_type=F32
        ).astype(BF16)


def back(first, place, offsets, pieces, chunks, parts, phases, basis, t_matrices, partials):
    count, m, size = partials[0].shape
    levels, rows, width = pieces[0].shape
    total_rows = basis.shape[0]
    group = 2
    steps = count // group * len(partials)

    def body(first_ref, place_ref, *refs):
        back_kernel(first_ref, place_ref, offsets, refs)

    def here(p, first, place):
        return (first[0] * steps + p if len(partials) == 1 else p, 0, 0)

    return pl.pallas_call(
        body,
        grid_spec=pltpu.PrefetchScalarGridSpec(
            num_scalar_prefetch=2,
            grid=(steps,),
            in_specs=[pl.BlockSpec((levels, rows, width), lambda p, *_: (0, 0, 0))] * len(pieces)
            + [
                pl.BlockSpec((group, 1, total_rows), here),
                pl.BlockSpec((total_rows, size), lambda p, *_: (0, 0)),
                pl.BlockSpec((group, size, size), here),
            ]
            + [pl.BlockSpec((group, m, size), lambda p, *_: (p % (count // group), 0, 0))]
            * len(partials),
            out_specs=pl.BlockSpec((group, m, size), lambda p, *_: (p, 0, 0)),
            scratch_shapes=[pltpu.VMEM((chunks, parts, rows, width), BF16)],
        ),
        out_shape=jax.ShapeDtypeStruct((steps * group, m, size), BF16),
        compiler_params=params(32),
        cost_estimate=cost(
            count * m * size * (total_rows + size), 2 * size * (total_rows + count * size)
        ),
        name="back",
    )(first, place, *pieces, phases, basis, t_matrices, *partials)


def local(
    incident,
    t_matrices,
    translations,
    near_index,
    near_count,
    near_type,
    phases,
    wave_basis,
    grating_blocks,
):
    doms, blks = lax.axis_size("dom"), lax.axis_size("blk")
    devices = doms * blks
    levels = min(4, blks)
    y_count = blks // levels
    x_lo = min(2, doms // 2)
    x_hi = doms // 2 // x_lo
    count, size, m = incident.shape
    reach = count // 2
    me = lax.axis_index(AXES)
    dom, blk = lax.axis_index("dom"), lax.axis_index("blk")
    core, x = dom % 2, dom // 2 % x_lo
    z, y = blk // y_count, blk % y_count
    parts = 2 * x_lo
    rows = m // parts

    def flip(array, mask):
        return lax.ppermute(array, AXES, [(i, i ^ mask) for i in range(devices)])

    def scalar(*values):
        return jnp.stack([jnp.asarray(v, jnp.int32) for v in values])

    core_mask, x_mask = blks, 2 * blks
    turns = [bin(dy).count("1") % 2 for dy in range(y_count)]
    y_masks = [turn * x_mask + dy for dy, turn in enumerate(turns)]
    twist = sum(jnp.where(y == dy, turn, 0) for dy, turn in enumerate(turns))
    offsets = [(dh, dy) for dh in (0, 1) for dy in range(y_count)]
    all_offsets = [(dc, dh, dy) for dc in (0, 1) for dh, dy in offsets]
    columns = [
        (h, d) for h in range(x_hi) for d in (2, 3, 1, 0) if d < levels and (h, d) != (0, 0)
    ]
    column_masks = [h * x_lo * 2 * blks + d * y_count for h, d in columns]
    place = scalar(x ^ twist, y, core)

    even = me % 2 == 0
    e_group = jnp.where(even, 1, 0).astype(jnp.int32)
    o_group = 1 - e_group
    e_pairs = [(i, i ^ 1) for i in range(devices)]
    o_pairs = [(i, i - 1 if i % 2 == 0 else i + 1) for i in range(1, devices - 1)]
    side = (near_index - me * count + reach) // reach
    within = (near_index - me * count + reach) % reach

    def lists(group):
        def taken(array):
            return lax.dynamic_slice_in_dim(array, group * reach, reach, axis=0)

        position = jnp.where(group == 0, side, 3 - side)
        slots = jnp.clip(position * reach + within, 0, 3 * reach - 1)
        return taken(slots).astype(jnp.int32), taken(near_count), taken(near_type)

    e_lists, o_lists = lists(e_group), lists(o_group)
    e_first, o_first = scalar(e_group), scalar(o_group)
    incident_t = jnp.swapaxes(incident, 1, 2)
    phase_rows = phases[:, None, :]
    grouped_phases = jnp.concatenate(
        [lax.dynamic_slice_in_dim(phases, g * reach, reach, axis=0) for g in (o_group, e_group)],
        axis=0,
    ).astype(F32)

    held = [pltpu.with_memory_space_constraint(a, pltpu.HBM) for a in (incident_t, t_matrices)]
    o_coeffs = solve(o_first, *held, reach)
    e_coeffs = solve(e_first, *held, reach)
    for sweep in range(ITERS):
        last = sweep == ITERS - 1
        o_halo = lax.ppermute(o_coeffs, AXES, o_pairs)
        common = ((o_coeffs, e_coeffs), wave_basis, grouped_phases, 2, blks)
        send = outward(scalar(1 - core), *common)
        got = flip(send, core_mask)
        keep = outward(scalar(core), *common)
        shape = (blks, x_lo, rows, keep.shape[2])
        mine, theirs = split(place, keep.reshape(shape), got.reshape(shape))
        pieces = deal(place, levels, mine, flip(theirs, x_mask))
        arrived = [flip(pieces[dy], y_masks[dy]) for dy in range(1, y_count)]
        if sweep == 0:
            own_blocks, _ = lax.optimization_barrier((grating_blocks.astype(BF16), mine))
            gathered = jnp.zeros((levels,) + own_blocks.shape, BF16)
            gathered = lax.dynamic_update_slice(gathered, own_blocks[None], (z, 0, 0, 0))
            for d in range(1, levels):
                gathered = lax.dynamic_update_slice(
                    gathered, flip(own_blocks, d * y_count)[None], (z ^ d, 0, 0, 0)
                )
        arrived, o_halo = lax.optimization_barrier((arrived, o_halo))
        plane_sum = add(pieces[0], *arrived)
        e_sent, _ = lax.optimization_barrier((e_coeffs, plane_sum))
        e_halo = lax.ppermute(e_sent, AXES, e_pairs)
        o_near = near(
            o_first, *o_lists, o_halo, o_coeffs, e_coeffs, incident_t, translations
        )
        arrived = [flip(plane_sum, mask) for mask in column_masks]
        arrived, o_near = lax.optimization_barrier((arrived, o_near))
        stack = reflect([plane_sum, *arrived], gathered)
        stacks = [stack] + [flip(stack, mask) for mask in y_masks[1:]]
        stacks = stacks + [flip(piece, x_mask) for piece in stacks]
        if last:
            stacks = stacks + [flip(piece, core_mask) for piece in stacks]
        e_near = near(
            e_first, *e_lists, e_halo, e_coeffs, o_coeffs, incident_t, translations
        )
        if not last:
            late = [n for n, (dh, dy) in enumerate(offsets) if dh and dy]
            held, e_near = lax.optimization_barrier(([stacks[n] for n in late], e_near))
            for n, piece in zip(late, held):
                stacks[n] = piece
            stacks = stacks + [flip(piece, core_mask) for piece in stacks]
        common = (place, all_offsets, stacks, blks, parts, phase_rows, wave_basis, t_matrices)
        if last:
            coeffs = back(o_first, *common, (o_near, e_near))
        else:
            o_coeffs = back(o_first, *common, (o_near,))
            e_near, _ = lax.optimization_barrier((e_near, o_coeffs))
            e_coeffs = back(e_first, *common, (e_near,))
    return jnp.swapaxes(coeffs, 1, 2)


def solution(mesh):
    placed = (
        P(("dom", "blk"), None, None),
        P(("dom", "blk"), None, None),
        P(),
        P(("dom", "blk"), None),
        P(("dom", "blk")),
        P(("dom", "blk"), None),
        P(("dom", "blk"), None),
        P(),
        P("blk", None, None),
    )
    return jax.shard_map(
        local, mesh=mesh, in_specs=placed, out_specs=P(("dom", "blk"), None, None), check_vma=False
    )
```

```python
import jax
import jax.numpy as jnp
from jax import lax
from jax.experimental import pallas as pl
from jax.experimental.pallas import tpu as pltpu
from jax.sharding import PartitionSpec as P

ITERS = 2
AXES = ("dom", "blk")
F32 = jnp.float32
BF16 = jnp.bfloat16
LAST = (((1,), (1,)), ((), ()))
MIB = 1 << 20


SCALARS = pl.BlockSpec(memory_space=pltpu.SMEM)
VECTORS = pl.BlockSpec(memory_space=pltpu.VMEM)
ANYWHERE = pl.BlockSpec(memory_space=pl.ANY)


def params(mib):
    return pltpu.CompilerParams(vmem_limit_bytes=mib * MIB)


def cost(macs, moved, real=False):
    if real:
        return pl.CostEstimate(flops=2 * macs, bytes_accessed=moved, transcendentals=0)
    return pl.CostEstimate(flops=1, bytes_accessed=1, transcendentals=0)


def solve_kernel(staged, first_ref, source_ref, t_ref, *refs):
    out_ref = refs[staged]
    sources, matrices, arrived, staging = refs[-4:]
    count = out_ref.shape[0]
    copies = []
    for p in range(count):
        at = first_ref[0] * count + p
        pair = (
            pltpu.make_async_copy(source_ref.at[at], sources.at[p], arrived.at[2 * p]),
            pltpu.make_async_copy(t_ref.at[at], matrices.at[p], arrived.at[2 * p + 1]),
        )
        for copy in pair:
            copy.start()
        copies.append(pair)
    moves = [
        pltpu.make_async_copy(refs[n], refs[staged + 1 + n], staging.at[n]) for n in range(staged)
    ]
    for move in moves:
        move.start()
    for p in range(count):
        for copy in copies[p]:
            copy.wait()
        out_ref[p] = lax.dot_general(
            sources[p], matrices[p], LAST, preferred_element_type=F32
        ).astype(BF16)
    for move in moves:
        move.wait()


def solve(first, source, t_matrices, count, staged=()):
    m, size = source.shape[1:]

    def body(*refs):
        solve_kernel(len(staged), *refs)

    return pl.pallas_call(
        body,
        in_specs=[SCALARS] + [ANYWHERE] * (2 + len(staged)),
        out_specs=[VECTORS] * (1 + len(staged)),
        scratch_shapes=[
            pltpu.VMEM((count, m, size), BF16),
            pltpu.VMEM((count, size, size), BF16),
            pltpu.SemaphoreType.DMA((2 * count,)),
            pltpu.SemaphoreType.DMA((max(1, len(staged)),)),
        ],
        out_shape=[jax.ShapeDtypeStruct((count, m, size), BF16)]
        + [jax.ShapeDtypeStruct(array.shape, array.dtype) for array in staged],
        compiler_params=params(12),
        cost_estimate=cost(count * m * size * size, 2 * count * size * (2 * m + size)),
        name="solve",
    )(first, source, t_matrices, *staged)


def outward_kernel(part_ref, *refs):
    pieces, (basis_ref, phase_ref, out_ref) = refs[:-3], refs[-3:]
    chunks, rows, chunk = out_ref.shape
    total_rows, size = basis_ref.shape
    width = min(1024, total_rows)
    start = pl.multiple_of(part_ref[0] * rows, 16)
    source = jnp.concatenate(
        [ref[:, pl.ds(start, rows), :].reshape(-1, size) for ref in pieces], axis=0
    )
    for g in range(0, total_rows, width):
        spread = lax.dot_general(
            source, basis_ref[g : g + width, :], LAST, preferred_element_type=F32
        )
        total = phase_ref[0:1, g : g + width] * spread[:rows]
        for p in range(1, phase_ref.shape[0]):
            total = total + phase_ref[p : p + 1, g : g + width] * spread[p * rows : (p + 1) * rows]
        total = total.astype(BF16)
        for c in range(0, width, chunk):
            out_ref[(g + c) // chunk] = total[:, c : c + chunk]


def outward(part, pieces, basis, phases, parts, chunks):
    m, size = pieces[0].shape[1:]
    count, total_rows = phases.shape
    chunk = total_rows // chunks
    rows = m // parts
    return pl.pallas_call(
        outward_kernel,
        in_specs=[SCALARS] + [VECTORS] * (len(pieces) + 2),
        out_specs=VECTORS,
        out_shape=jax.ShapeDtypeStruct((chunks, rows, chunk), BF16),
        compiler_params=params(16),
        cost_estimate=cost(count * rows * size * total_rows, 2 * size * total_rows),
        name="outward",
    )(part, *pieces, basis, phases)


def split_kernel(place_ref, keep_ref, got_ref, here_ref, there_ref):
    for dx, out_ref in ((0, here_ref), (1, there_ref)):
        x = place_ref[0] ^ dx
        for chunk in range(keep_ref.shape[0]):
            out_ref[chunk] = (
                keep_ref[chunk, x].astype(F32) + got_ref[chunk, x].astype(F32)
            ).astype(BF16)


def split(place, keep, got):
    chunks, _, rows, width = keep.shape
    return pl.pallas_call(
        split_kernel,
        in_specs=[SCALARS, VECTORS, VECTORS],
        out_specs=[VECTORS] * 2,
        out_shape=[jax.ShapeDtypeStruct((chunks, rows, width), BF16)] * 2,
        compiler_params=params(4),
        cost_estimate=cost(keep.size, 6 * keep.size),
        name="split",
    )(place, keep, got)


def deal_kernel(place_ref, mine_ref, got_ref, *out_refs):
    levels = out_refs[0].shape[0]
    across = mine_ref.shape[0] // levels
    for dy, out_ref in enumerate(out_refs):
        for level in range(levels):
            chunk = level * across + (place_ref[1] ^ dy)
            out_ref[level] = (
                mine_ref[chunk].astype(F32) + got_ref[chunk].astype(F32)
            ).astype(BF16)


def deal(place, levels, mine, got):
    chunks, rows, width = mine.shape
    across = chunks // levels
    return pl.pallas_call(
        deal_kernel,
        in_specs=[SCALARS, VECTORS, VECTORS],
        out_specs=[VECTORS] * across,
        out_shape=[jax.ShapeDtypeStruct((levels, rows, width), BF16)] * across,
        compiler_params=params(4),
        cost_estimate=cost(mine.size, 6 * mine.size),
        name="deal",
    )(place, mine, got)


def add_kernel(*refs):
    total = refs[0][...].astype(F32)
    for ref in refs[1:-1]:
        total = total + ref[...].astype(F32)
    refs[-1][...] = total.astype(BF16)


def add(*terms):
    return pl.pallas_call(
        add_kernel,
        out_shape=jax.ShapeDtypeStruct(terms[0].shape, BF16),
        compiler_params=params(8),
        cost_estimate=cost(len(terms) * terms[0].size, 2 * (len(terms) + 1) * terms[0].size),
        name="add",
    )(*terms)


def reflect_kernel(*refs):
    blocks_ref, out_ref = refs[-2:]
    levels, owned, order = blocks_ref.shape[:3]
    total = refs[0][...].astype(F32)
    for ref in refs[1:-2]:
        total = total + ref[...].astype(F32)
    total = total.astype(BF16)
    for level in range(levels):
        for b in range(owned):
            out_ref[level, :, b * order : (b + 1) * order] = lax.dot_general(
                total[level, :, b * order : (b + 1) * order],
                blocks_ref[level, b],
                LAST,
                preferred_element_type=F32,
            ).astype(BF16)


def reflect(terms, blocks):
    return pl.pallas_call(
        reflect_kernel,
        out_shape=jax.ShapeDtypeStruct(terms[0].shape, BF16),
        compiler_params=params(8),
        cost_estimate=cost(terms[0].size * 128, 2 * (len(terms) + 1) * terms[0].size),
        name="reflect",
    )(*terms, blocks)


def near_kernel(
    first_ref,
    slot_ref,
    count_ref,
    type_ref,
    halo_ref,
    own_ref,
    inner_ref,
    incident_ref,
    translations_ref,
    out_ref,
    extended,
    sums,
):
    group, m, size = incident_ref.shape
    kinds = translations_ref.shape[0]
    most = slot_ref.shape[1]
    for index, ref in enumerate((halo_ref, own_ref, inner_ref)):
        extended[pl.ds(index * group, group)] = ref[...]
    sums[...] = jnp.zeros(sums.shape, F32)
    for p in range(group):
        for k in range(most):

            @pl.when(k < count_ref[p])
            def _():
                place = type_ref[p, k]
                sums[place, p] += extended[slot_ref[p, k]].astype(F32)

    total = incident_ref[...].astype(F32).reshape(group * m, size)
    for t in range(kinds):
        total = total + lax.dot_general(
            sums[t].astype(BF16).reshape(group * m, size),
            translations_ref[t],
            LAST,
            preferred_element_type=F32,
        )
    out_ref[...] = total.reshape(group, m, size)


def near(first, slots, counts, types, halo, own, inner, incident, translations):
    m, size = incident.shape[1:]
    group = own.shape[0]
    kinds = translations.shape[0]
    whole = pl.BlockSpec((group, m, size), lambda p, *_: (0, 0, 0))
    return pl.pallas_call(
        near_kernel,
        grid_spec=pltpu.PrefetchScalarGridSpec(
            num_scalar_prefetch=4,
            grid=(1,),
            in_specs=[
                whole,
                whole,
                whole,
                pl.BlockSpec((group, m, size), lambda p, first, *_: (first[0], 0, 0)),
                pl.BlockSpec((kinds, size, size), lambda p, *_: (0, 0, 0)),
            ],
            out_specs=whole,
            scratch_shapes=[
                pltpu.VMEM((3 * group, m, size), BF16),
                pltpu.VMEM((kinds, group, m, size), F32),
            ],
        ),
        out_shape=jax.ShapeDtypeStruct((group, m, size), F32),
        compiler_params=params(32),
        cost_estimate=cost(kinds * group * m * size * size, 2 * size * size * kinds),
        name="near",
    )(first, slots, counts, types, halo, own, inner, incident, translations)


def back_kernel(first_ref, place_ref, offsets, refs):
    pieces = refs[: len(offsets)]
    phase_ref, basis_ref, t_ref = refs[len(offsets) : len(offsets) + 3]
    partials = refs[len(offsets) + 3 : -2]
    out_ref, waves = refs[-2:]
    group, m, size = out_ref.shape
    chunks, parts, rows, width = waves.shape
    levels = pieces[0].shape[0]
    across = chunks // levels

    @pl.when(pl.program_id(0) == 0)
    def _():
        for (dc, dx, dy), piece in zip(offsets, pieces):
            part = (place_ref[2] ^ dc) * (parts // 2) + (place_ref[0] ^ dx)
            for level in range(levels):
                waves[level * across + (place_ref[1] ^ dy), part] = piece[level]

    total = partials[0][...]
    if len(partials) > 1:
        total = jnp.where(pl.program_id(0) == first_ref[0], total, partials[1][...])
    total = total.reshape(group * m, size)
    for c in range(chunks):
        waves_here = waves[c].reshape(m, width)
        weighted = [
            phase_ref[i, :, pl.ds(c * width, width)] * waves_here for i in range(group)
        ]
        total = total + jnp.dot(
            jnp.concatenate(weighted, axis=0),
            basis_ref[pl.ds(c * width, width), :],
            preferred_element_type=F32,
        )
    source = total.astype(BF16)
    for i in range(group):
        out_ref[i] = lax.dot_general(
            source[i * m : (i + 1) * m], t_ref[i], LAST, preferred_element_type=F32
        ).astype(BF16)


def back(first, place, offsets, pieces, chunks, parts, phases, basis, t_matrices, partials):
    count, m, size = partials[0].shape
    levels, rows, width = pieces[0].shape
    total_rows = basis.shape[0]
    group = 2 if len(partials) == 1 else count
    steps = count // group * len(partials)

    def body(first_ref, place_ref, *refs):
        back_kernel(first_ref, place_ref, offsets, refs)

    def here(p, first, place):
        return (first[0] * steps + p if len(partials) == 1 else p, 0, 0)

    return pl.pallas_call(
        body,
        grid_spec=pltpu.PrefetchScalarGridSpec(
            num_scalar_prefetch=2,
            grid=(steps,),
            in_specs=[pl.BlockSpec((levels, rows, width), lambda p, *_: (0, 0, 0))] * len(pieces)
            + [
                pl.BlockSpec((group, 1, total_rows), here),
                pl.BlockSpec((total_rows, size), lambda p, *_: (0, 0)),
                pl.BlockSpec((group, size, size), here),
            ]
            + [pl.BlockSpec((group, m, size), lambda p, *_: (p % (count // group), 0, 0))]
            * len(partials),
            out_specs=pl.BlockSpec((group, m, size), lambda p, *_: (p, 0, 0)),
            scratch_shapes=[pltpu.VMEM((chunks, parts, rows, width), BF16)],
        ),
        out_shape=jax.ShapeDtypeStruct((steps * group, m, size), BF16),
        compiler_params=params(32),
        cost_estimate=cost(
            count * m * size * (total_rows + size), 2 * size * (total_rows + count * size)
        ),
        name="back",
    )(first, place, *pieces, phases, basis, t_matrices, *partials)


def local(
    incident,
    t_matrices,
    translations,
    near_index,
    near_count,
    near_type,
    phases,
    wave_basis,
    grating_blocks,
):
    doms, blks = lax.axis_size("dom"), lax.axis_size("blk")
    devices = doms * blks
    levels = min(4, blks)
    y_count = blks // levels
    x_lo = min(2, doms // 2)
    x_hi = doms // 2 // x_lo
    count, size, m = incident.shape
    reach = count // 2
    me = lax.axis_index(AXES)
    dom, blk = lax.axis_index("dom"), lax.axis_index("blk")
    core, x = dom % 2, dom // 2 % x_lo
    z, y = blk // y_count, blk % y_count
    parts = 2 * x_lo
    rows = m // parts

    def flip(array, mask):
        return lax.ppermute(array, AXES, [(i, i ^ mask) for i in range(devices)])

    def scalar(*values):
        return jnp.stack([jnp.asarray(v, jnp.int32) for v in values])

    core_mask, x_mask = blks, 2 * blks
    turns = [bin(dy).count("1") % 2 for dy in range(y_count)]
    y_masks = [turn * x_mask + dy for dy, turn in enumerate(turns)]
    twist = sum(jnp.where(y == dy, turn, 0) for dy, turn in enumerate(turns))
    offsets = [(dh, dy) for dh in (0, 1) for dy in range(y_count)]
    all_offsets = [(dc, dh, dy) for dc in (0, 1) for dh, dy in offsets]
    columns = [
        (h, d) for h in range(x_hi) for d in (2, 3, 1, 0) if d < levels and (h, d) != (0, 0)
    ]
    column_masks = [h * x_lo * 2 * blks + d * y_count for h, d in columns]
    place = scalar(x ^ twist, y, core)

    even = me % 2 == 0
    e_group = jnp.where(even, 1, 0).astype(jnp.int32)
    o_group = 1 - e_group
    e_pairs = [(i, i ^ 1) for i in range(devices)]
    o_pairs = [(i, i - 1 if i % 2 == 0 else i + 1) for i in range(1, devices - 1)]
    side = (near_index - me * count + reach) // reach
    within = (near_index - me * count + reach) % reach

    def lists(group):
        def taken(array):
            return lax.dynamic_slice_in_dim(array, group * reach, reach, axis=0)

        position = jnp.where(group == 0, side, 3 - side)
        slots = jnp.clip(position * reach + within, 0, 3 * reach - 1)
        return taken(slots).astype(jnp.int32), taken(near_count), taken(near_type)

    e_lists, o_lists = lists(e_group), lists(o_group)
    e_first, o_first = scalar(e_group), scalar(o_group)
    incident_t = jnp.swapaxes(incident, 1, 2)
    phase_rows = phases[:, None, :]
    grouped_phases = jnp.concatenate(
        [lax.dynamic_slice_in_dim(phases, g * reach, reach, axis=0) for g in (o_group, e_group)],
        axis=0,
    ).astype(F32)

    held = [pltpu.with_memory_space_constraint(a, pltpu.HBM) for a in (incident_t, t_matrices)]
    wave_basis = pltpu.with_memory_space_constraint(wave_basis, pltpu.HBM)
    translations = pltpu.with_memory_space_constraint(translations, pltpu.HBM)
    (o_coeffs,) = solve(o_first, *held, reach)
    e_coeffs, wave_basis, translations = solve(
        e_first, *held, reach, (wave_basis, translations,)
    )
    for sweep in range(ITERS):
        last = sweep == ITERS - 1
        o_halo = lax.ppermute(o_coeffs, AXES, o_pairs)
        common = ((o_coeffs, e_coeffs), wave_basis, grouped_phases, 2, blks)
        send = outward(scalar(1 - core), *common)
        got = flip(send, core_mask)
        keep = outward(scalar(core), *common)
        shape = (blks, x_lo, rows, keep.shape[2])
        mine, theirs = split(place, keep.reshape(shape), got.reshape(shape))
        pieces = deal(place, levels, mine, flip(theirs, x_mask))
        arrived = [flip(pieces[dy], y_masks[dy]) for dy in range(1, y_count)]
        if sweep == 0:
            own_blocks, _ = lax.optimization_barrier((grating_blocks.astype(BF16), mine))
            gathered = jnp.zeros((levels,) + own_blocks.shape, BF16)
            gathered = lax.dynamic_update_slice(gathered, own_blocks[None], (z, 0, 0, 0))
            for d in range(1, levels):
                gathered = lax.dynamic_update_slice(
                    gathered, flip(own_blocks, d * y_count)[None], (z ^ d, 0, 0, 0)
                )
        arrived, o_halo = lax.optimization_barrier((arrived, o_halo))
        plane_sum = add(pieces[0], *arrived)
        e_sent, _ = lax.optimization_barrier((e_coeffs, plane_sum))
        e_halo = lax.ppermute(e_sent, AXES, e_pairs)
        o_near = near(
            o_first, *o_lists, o_halo, o_coeffs, e_coeffs, incident_t, translations
        )
        arrived = [flip(plane_sum, mask) for mask in column_masks]
        arrived, o_near = lax.optimization_barrier((arrived, o_near))
        stack = reflect([plane_sum, *arrived], gathered)
        stacks = [stack] + [flip(stack, mask) for mask in y_masks[1:]]
        stacks = stacks + [flip(piece, x_mask) for piece in stacks]
        if last:
            stacks = stacks + [flip(piece, core_mask) for piece in stacks]
        e_near = near(
            e_first, *e_lists, e_halo, e_coeffs, o_coeffs, incident_t, translations
        )
        if not last:
            late = [n for n, (dh, dy) in enumerate(offsets) if dh and dy]
            held, e_near = lax.optimization_barrier(([stacks[n] for n in late], e_near))
            for n, piece in zip(late, held):
                stacks[n] = piece
            stacks = stacks + [flip(piece, core_mask) for piece in stacks]
        common = (place, all_offsets, stacks, blks, parts, phase_rows, wave_basis, t_matrices)
        if last:
            coeffs = back(o_first, *common, (o_near, e_near))
        else:
            o_coeffs = back(o_first, *common, (o_near,))
            e_near, _ = lax.optimization_barrier((e_near, o_coeffs))
            e_coeffs = back(e_first, *common, (e_near,))
    return jnp.swapaxes(coeffs, 1, 2)


def solution(mesh):
    placed = (
        P(("dom", "blk"), None, None),
        P(("dom", "blk"), None, None),
        P(),
        P(("dom", "blk"), None),
        P(("dom", "blk")),
        P(("dom", "blk"), None),
        P(("dom", "blk"), None),
        P(),
        P("blk", None, None),
    )
    return jax.shard_map(
        local, mesh=mesh, in_specs=placed, out_specs=P(("dom", "blk"), None, None), check_vma=False
    )
```

```python
import jax
import jax.numpy as jnp
from jax import lax
from jax.experimental import pallas as pl
from jax.experimental.pallas import tpu as pltpu
from jax.sharding import PartitionSpec as P

ITERS = 2
AXES = ("dom", "blk")
F32 = jnp.float32
BF16 = jnp.bfloat16
LAST = (((1,), (1,)), ((), ()))
MIB = 1 << 20


SCALARS = pl.BlockSpec(memory_space=pltpu.SMEM)
VECTORS = pl.BlockSpec(memory_space=pltpu.VMEM)
ANYWHERE = pl.BlockSpec(memory_space=pl.ANY)


def params(mib):
    return pltpu.CompilerParams(vmem_limit_bytes=mib * MIB)


def cost(macs, moved, real=False):
    if real:
        return pl.CostEstimate(flops=2 * macs, bytes_accessed=moved, transcendentals=0)
    return pl.CostEstimate(flops=1, bytes_accessed=1, transcendentals=0)


def solve_kernel(staged, first_ref, source_ref, t_ref, *refs):
    out_ref = refs[staged]
    sources, matrices, arrived, staging = refs[-4:]
    count = out_ref.shape[0]
    copies = []
    for p in range(count):
        at = first_ref[0] * count + p
        pair = (
            pltpu.make_async_copy(source_ref.at[at], sources.at[p], arrived.at[2 * p]),
            pltpu.make_async_copy(t_ref.at[at], matrices.at[p], arrived.at[2 * p + 1]),
        )
        for copy in pair:
            copy.start()
        copies.append(pair)
    moves = [
        pltpu.make_async_copy(refs[n], refs[staged + 1 + n], staging.at[n]) for n in range(staged)
    ]
    for move in moves:
        move.start()
    for p in range(count):
        for copy in copies[p]:
            copy.wait()
        out_ref[p] = lax.dot_general(
            sources[p], matrices[p], LAST, preferred_element_type=F32
        ).astype(BF16)
    for move in moves:
        move.wait()


def solve(first, source, t_matrices, count, staged=()):
    m, size = source.shape[1:]

    def body(*refs):
        solve_kernel(len(staged), *refs)

    return pl.pallas_call(
        body,
        in_specs=[SCALARS] + [ANYWHERE] * (2 + len(staged)),
        out_specs=[VECTORS] * (1 + len(staged)),
        scratch_shapes=[
            pltpu.VMEM((count, m, size), BF16),
            pltpu.VMEM((count, size, size), BF16),
            pltpu.SemaphoreType.DMA((2 * count,)),
            pltpu.SemaphoreType.DMA((max(1, len(staged)),)),
        ],
        out_shape=[jax.ShapeDtypeStruct((count, m, size), BF16)]
        + [jax.ShapeDtypeStruct(array.shape, array.dtype) for array in staged],
        compiler_params=params(12),
        cost_estimate=cost(count * m * size * size, 2 * count * size * (2 * m + size), real=True),
        name="solve",
    )(first, source, t_matrices, *staged)


def outward_kernel(part_ref, *refs):
    pieces, (basis_ref, phase_ref, out_ref) = refs[:-3], refs[-3:]
    chunks, rows, chunk = out_ref.shape
    total_rows, size = basis_ref.shape
    width = min(1024, total_rows)
    start = pl.multiple_of(part_ref[0] * rows, 16)
    source = jnp.concatenate(
        [ref[:, pl.ds(start, rows), :].reshape(-1, size) for ref in pieces], axis=0
    )
    for g in range(0, total_rows, width):
        spread = lax.dot_general(
            source, basis_ref[g : g + width, :], LAST, preferred_element_type=F32
        )
        total = phase_ref[0:1, g : g + width] * spread[:rows]
        for p in range(1, phase_ref.shape[0]):
            total = total + phase_ref[p : p + 1, g : g + width] * spread[p * rows : (p + 1) * rows]
        total = total.astype(BF16)
        for c in range(0, width, chunk):
            out_ref[(g + c) // chunk] = total[:, c : c + chunk]


def outward(part, pieces, basis, phases, parts, chunks):
    m, size = pieces[0].shape[1:]
    count, total_rows = phases.shape
    chunk = total_rows // chunks
    rows = m // parts
    return pl.pallas_call(
        outward_kernel,
        in_specs=[SCALARS] + [VECTORS] * (len(pieces) + 2),
        out_specs=VECTORS,
        out_shape=jax.ShapeDtypeStruct((chunks, rows, chunk), BF16),
        compiler_params=params(16),
        cost_estimate=cost(count * rows * size * total_rows, 2 * size * total_rows),
        name="outward",
    )(part, *pieces, basis, phases)


def split_kernel(place_ref, keep_ref, got_ref, here_ref, there_ref):
    for dx, out_ref in ((0, here_ref), (1, there_ref)):
        x = place_ref[0] ^ dx
        for chunk in range(keep_ref.shape[0]):
            out_ref[chunk] = (
                keep_ref[chunk, x].astype(F32) + got_ref[chunk, x].astype(F32)
            ).astype(BF16)


def split(place, keep, got):
    chunks, _, rows, width = keep.shape
    return pl.pallas_call(
        split_kernel,
        in_specs=[SCALARS, VECTORS, VECTORS],
        out_specs=[VECTORS] * 2,
        out_shape=[jax.ShapeDtypeStruct((chunks, rows, width), BF16)] * 2,
        compiler_params=params(4),
        cost_estimate=cost(keep.size, 6 * keep.size),
        name="split",
    )(place, keep, got)


def deal_kernel(place_ref, mine_ref, got_ref, *out_refs):
    levels = out_refs[0].shape[0]
    across = mine_ref.shape[0] // levels
    for dy, out_ref in enumerate(out_refs):
        for level in range(levels):
            chunk = level * across + (place_ref[1] ^ dy)
            out_ref[level] = (
                mine_ref[chunk].astype(F32) + got_ref[chunk].astype(F32)
            ).astype(BF16)


def deal(place, levels, mine, got):
    chunks, rows, width = mine.shape
    across = chunks // levels
    return pl.pallas_call(
        deal_kernel,
        in_specs=[SCALARS, VECTORS, VECTORS],
        out_specs=[VECTORS] * across,
        out_shape=[jax.ShapeDtypeStruct((levels, rows, width), BF16)] * across,
        compiler_params=params(4),
        cost_estimate=cost(mine.size, 6 * mine.size),
        name="deal",
    )(place, mine, got)


def add_kernel(*refs):
    total = refs[0][...].astype(F32)
    for ref in refs[1:-1]:
        total = total + ref[...].astype(F32)
    refs[-1][...] = total.astype(BF16)


def add(*terms):
    return pl.pallas_call(
        add_kernel,
        out_shape=jax.ShapeDtypeStruct(terms[0].shape, BF16),
        compiler_params=params(8),
        cost_estimate=cost(len(terms) * terms[0].size, 2 * (len(terms) + 1) * terms[0].size),
        name="add",
    )(*terms)


def reflect_kernel(*refs):
    blocks_ref, out_ref = refs[-2:]
    levels, owned, order = blocks_ref.shape[:3]
    total = refs[0][...].astype(F32)
    for ref in refs[1:-2]:
        total = total + ref[...].astype(F32)
    total = total.astype(BF16)
    for level in range(levels):
        for b in range(owned):
            out_ref[level, :, b * order : (b + 1) * order] = lax.dot_general(
                total[level, :, b * order : (b + 1) * order],
                blocks_ref[level, b],
                LAST,
                preferred_element_type=F32,
            ).astype(BF16)


def reflect(terms, blocks):
    return pl.pallas_call(
        reflect_kernel,
        out_shape=jax.ShapeDtypeStruct(terms[0].shape, BF16),
        compiler_params=params(8),
        cost_estimate=cost(terms[0].size * 128, 2 * (len(terms) + 1) * terms[0].size),
        name="reflect",
    )(*terms, blocks)


def near_kernel(
    first_ref,
    slot_ref,
    count_ref,
    type_ref,
    halo_ref,
    own_ref,
    inner_ref,
    incident_ref,
    translations_ref,
    out_ref,
    extended,
    sums,
):
    group, m, size = incident_ref.shape
    kinds = translations_ref.shape[0]
    most = slot_ref.shape[1]
    for index, ref in enumerate((halo_ref, own_ref, inner_ref)):
        extended[pl.ds(index * group, group)] = ref[...]
    sums[...] = jnp.zeros(sums.shape, F32)
    for p in range(group):
        for k in range(most):

            @pl.when(k < count_ref[p])
            def _():
                place = type_ref[p, k]
                sums[place, p] += extended[slot_ref[p, k]].astype(F32)

    total = incident_ref[...].astype(F32).reshape(group * m, size)
    for t in range(kinds):
        total = total + lax.dot_general(
            sums[t].astype(BF16).reshape(group * m, size),
            translations_ref[t],
            LAST,
            preferred_element_type=F32,
        )
    out_ref[...] = total.reshape(group, m, size)


def near(first, slots, counts, types, halo, own, inner, incident, translations):
    m, size = incident.shape[1:]
    group = own.shape[0]
    kinds = translations.shape[0]
    whole = pl.BlockSpec((group, m, size), lambda p, *_: (0, 0, 0))
    return pl.pallas_call(
        near_kernel,
        grid_spec=pltpu.PrefetchScalarGridSpec(
            num_scalar_prefetch=4,
            grid=(1,),
            in_specs=[
                whole,
                whole,
                whole,
                pl.BlockSpec((group, m, size), lambda p, first, *_: (first[0], 0, 0)),
                pl.BlockSpec((kinds, size, size), lambda p, *_: (0, 0, 0)),
            ],
            out_specs=whole,
            scratch_shapes=[
                pltpu.VMEM((3 * group, m, size), BF16),
                pltpu.VMEM((kinds, group, m, size), F32),
            ],
        ),
        out_shape=jax.ShapeDtypeStruct((group, m, size), F32),
        compiler_params=params(32),
        cost_estimate=cost(kinds * group * m * size * size, 2 * size * size * kinds, real=True),
        name="near",
    )(first, slots, counts, types, halo, own, inner, incident, translations)


def back_kernel(first_ref, place_ref, offsets, refs):
    pieces = refs[: len(offsets)]
    phase_ref, basis_ref, t_ref = refs[len(offsets) : len(offsets) + 3]
    partials = refs[len(offsets) + 3 : -2]
    out_ref, waves = refs[-2:]
    group, m, size = out_ref.shape
    chunks, parts, rows, width = waves.shape
    levels = pieces[0].shape[0]
    across = chunks // levels

    @pl.when(pl.program_id(0) == 0)
    def _():
        for (dc, dx, dy), piece in zip(offsets, pieces):
            part = (place_ref[2] ^ dc) * (parts // 2) + (place_ref[0] ^ dx)
            for level in range(levels):
                waves[level * across + (place_ref[1] ^ dy), part] = piece[level]

    total = partials[0][...]
    if len(partials) > 1:
        total = jnp.where(pl.program_id(0) == first_ref[0], total, partials[1][...])
    total = total.reshape(group * m, size)
    for c in range(chunks):
        waves_here = waves[c].reshape(m, width)
        weighted = [
            phase_ref[i, :, pl.ds(c * width, width)] * waves_here for i in range(group)
        ]
        total = total + jnp.dot(
            jnp.concatenate(weighted, axis=0),
            basis_ref[pl.ds(c * width, width), :],
            preferred_element_type=F32,
        )
    source = total.astype(BF16)
    for i in range(group):
        out_ref[i] = lax.dot_general(
            source[i * m : (i + 1) * m], t_ref[i], LAST, preferred_element_type=F32
        ).astype(BF16)


def back(first, place, offsets, pieces, chunks, parts, phases, basis, t_matrices, partials):
    count, m, size = partials[0].shape
    levels, rows, width = pieces[0].shape
    total_rows = basis.shape[0]
    group = 2 if len(partials) == 1 else count
    steps = count // group * len(partials)

    def body(first_ref, place_ref, *refs):
        back_kernel(first_ref, place_ref, offsets, refs)

    def here(p, first, place):
        return (first[0] * steps + p if len(partials) == 1 else p, 0, 0)

    return pl.pallas_call(
        body,
        grid_spec=pltpu.PrefetchScalarGridSpec(
            num_scalar_prefetch=2,
            grid=(steps,),
            in_specs=[pl.BlockSpec((levels, rows, width), lambda p, *_: (0, 0, 0))] * len(pieces)
            + [
                pl.BlockSpec((group, 1, total_rows), here),
                pl.BlockSpec((total_rows, size), lambda p, *_: (0, 0)),
                pl.BlockSpec((group, size, size), here),
            ]
            + [pl.BlockSpec((group, m, size), lambda p, *_: (p % (count // group), 0, 0))]
            * len(partials),
            out_specs=pl.BlockSpec((group, m, size), lambda p, *_: (p, 0, 0)),
            scratch_shapes=[pltpu.VMEM((chunks, parts, rows, width), BF16)],
        ),
        out_shape=jax.ShapeDtypeStruct((steps * group, m, size), BF16),
        compiler_params=params(32),
        cost_estimate=cost(
            count * m * size * (total_rows + size), 2 * size * (total_rows + count * size)
        ),
        name="back",
    )(first, place, *pieces, phases, basis, t_matrices, *partials)


def local(
    incident,
    t_matrices,
    translations,
    near_index,
    near_count,
    near_type,
    phases,
    wave_basis,
    grating_blocks,
):
    doms, blks = lax.axis_size("dom"), lax.axis_size("blk")
    devices = doms * blks
    levels = min(4, blks)
    y_count = blks // levels
    x_lo = min(2, doms // 2)
    x_hi = doms // 2 // x_lo
    count, size, m = incident.shape
    reach = count // 2
    me = lax.axis_index(AXES)
    dom, blk = lax.axis_index("dom"), lax.axis_index("blk")
    core, x = dom % 2, dom // 2 % x_lo
    z, y = blk // y_count, blk % y_count
    parts = 2 * x_lo
    rows = m // parts

    def flip(array, mask):
        return lax.ppermute(array, AXES, [(i, i ^ mask) for i in range(devices)])

    def scalar(*values):
        return jnp.stack([jnp.asarray(v, jnp.int32) for v in values])

    core_mask, x_mask = blks, 2 * blks
    turns = [bin(dy).count("1") % 2 for dy in range(y_count)]
    y_masks = [turn * x_mask + dy for dy, turn in enumerate(turns)]
    twist = sum(jnp.where(y == dy, turn, 0) for dy, turn in enumerate(turns))
    offsets = [(dh, dy) for dh in (0, 1) for dy in range(y_count)]
    all_offsets = [(dc, dh, dy) for dc in (0, 1) for dh, dy in offsets]
    columns = [
        (h, d) for h in range(x_hi) for d in (2, 3, 1, 0) if d < levels and (h, d) != (0, 0)
    ]
    column_masks = [h * x_lo * 2 * blks + d * y_count for h, d in columns]
    place = scalar(x ^ twist, y, core)

    even = me % 2 == 0
    e_group = jnp.where(even, 1, 0).astype(jnp.int32)
    o_group = 1 - e_group
    e_pairs = [(i, i ^ 1) for i in range(devices)]
    o_pairs = [(i, i - 1 if i % 2 == 0 else i + 1) for i in range(1, devices - 1)]
    side = (near_index - me * count + reach) // reach
    within = (near_index - me * count + reach) % reach

    def lists(group):
        def taken(array):
            return lax.dynamic_slice_in_dim(array, group * reach, reach, axis=0)

        position = jnp.where(group == 0, side, 3 - side)
        slots = jnp.clip(position * reach + within, 0, 3 * reach - 1)
        return taken(slots).astype(jnp.int32), taken(near_count), taken(near_type)

    e_lists, o_lists = lists(e_group), lists(o_group)
    e_first, o_first = scalar(e_group), scalar(o_group)
    incident_t = jnp.swapaxes(incident, 1, 2)
    phase_rows = phases[:, None, :]
    grouped_phases = jnp.concatenate(
        [lax.dynamic_slice_in_dim(phases, g * reach, reach, axis=0) for g in (o_group, e_group)],
        axis=0,
    ).astype(F32)

    held = [pltpu.with_memory_space_constraint(a, pltpu.HBM) for a in (incident_t, t_matrices)]
    wave_basis = pltpu.with_memory_space_constraint(wave_basis, pltpu.HBM)
    translations = pltpu.with_memory_space_constraint(translations, pltpu.HBM)
    (o_coeffs,) = solve(o_first, *held, reach)
    e_coeffs, wave_basis, translations = solve(
        e_first, *held, reach, (wave_basis, translations,)
    )
    for sweep in range(ITERS):
        last = sweep == ITERS - 1
        o_halo = lax.ppermute(o_coeffs, AXES, o_pairs)
        common = ((o_coeffs, e_coeffs), wave_basis, grouped_phases, 2, blks)
        send = outward(scalar(1 - core), *common)
        got = flip(send, core_mask)
        keep = outward(scalar(core), *common)
        shape = (blks, x_lo, rows, keep.shape[2])
        mine, theirs = split(place, keep.reshape(shape), got.reshape(shape))
        pieces = deal(place, levels, mine, flip(theirs, x_mask))
        arrived = [flip(pieces[dy], y_masks[dy]) for dy in range(1, y_count)]
        if sweep == 0:
            own_blocks, _ = lax.optimization_barrier((grating_blocks.astype(BF16), mine))
            gathered = jnp.zeros((levels,) + own_blocks.shape, BF16)
            gathered = lax.dynamic_update_slice(gathered, own_blocks[None], (z, 0, 0, 0))
            for d in range(1, levels):
                gathered = lax.dynamic_update_slice(
                    gathered, flip(own_blocks, d * y_count)[None], (z ^ d, 0, 0, 0)
                )
        arrived, o_halo = lax.optimization_barrier((arrived, o_halo))
        plane_sum = add(pieces[0], *arrived)
        e_sent, _ = lax.optimization_barrier((e_coeffs, plane_sum))
        e_halo = lax.ppermute(e_sent, AXES, e_pairs)
        o_near = near(
            o_first, *o_lists, o_halo, o_coeffs, e_coeffs, incident_t, translations
        )
        arrived = [flip(plane_sum, mask) for mask in column_masks]
        arrived, o_near = lax.optimization_barrier((arrived, o_near))
        stack = reflect([plane_sum, *arrived], gathered)
        stacks = [stack] + [flip(stack, mask) for mask in y_masks[1:]]
        stacks = stacks + [flip(piece, x_mask) for piece in stacks]
        if last:
            stacks = stacks + [flip(piece, core_mask) for piece in stacks]
        e_near = near(
            e_first, *e_lists, e_halo, e_coeffs, o_coeffs, incident_t, translations
        )
        if not last:
            late = [n for n, (dh, dy) in enumerate(offsets) if dh and dy]
            held, e_near = lax.optimization_barrier(([stacks[n] for n in late], e_near))
            for n, piece in zip(late, held):
                stacks[n] = piece
            stacks = stacks + [flip(piece, core_mask) for piece in stacks]
        common = (place, all_offsets, stacks, blks, parts, phase_rows, wave_basis, t_matrices)
        if last:
            coeffs = back(o_first, *common, (o_near, e_near))
        else:
            o_coeffs = back(o_first, *common, (o_near,))
            e_near, _ = lax.optimization_barrier((e_near, o_coeffs))
            e_coeffs = back(e_first, *common, (e_near,))
    return jnp.swapaxes(coeffs, 1, 2)


def solution(mesh):
    placed = (
        P(("dom", "blk"), None, None),
        P(("dom", "blk"), None, None),
        P(),
        P(("dom", "blk"), None),
        P(("dom", "blk")),
        P(("dom", "blk"), None),
        P(("dom", "blk"), None),
        P(),
        P("blk", None, None),
    )
    return jax.shard_map(
        local, mesh=mesh, in_specs=placed, out_specs=P(("dom", "blk"), None, None), check_vma=False
    )
```
